1024 devices in a mesh: narrow: 64 (over x, z), wide: 16 (over y, core).
Axes of the slice: x: 8, y: 8, z: 8, core: 2. Of those that a mesh axis runs over, the one named last changes fastest.
Arguments:
- flow_state: float32 [19, 512, 128, 128], P(None, 'narrow', 'wide'), as said below
- thermal_distributions_current: float32 [7, 512, 128, 128], P(None, 'narrow', 'wide'), as said below
- fluid_mask: int32 [512, 128, 128], P('narrow', 'wide'), may hold values 0 or 1
- heat_rate: float32 [512, 128, 128], P('narrow', 'wide'), may hold values from 0.6 to 1.8
- solid_source: float32 [1024, 16, 256], P(('narrow', 'wide')), may hold values from -6 to 6
- cube_uptake_coefficients: float32 [1024], P(('narrow', 'wide')), may hold values from 0.05 to 0.5
- owner_of: int32 [262144, 1], P(('narrow', 'wide')), may hold values from 0 to 63; in each aligned block of 256 rows (0 to 255, 256 to 511, ...) at most 16 rows name the same one
- emitting_grid_site: int32 [262144], P(('narrow', 'wide')), may hold values from 0 to 8191
- target_node: int32 [262144], P(('narrow', 'wide')), may hold values from 0 to 255
Outputs:
- stream_distributions_after: float32 [19, 512, 128, 128], P(None, 'narrow', 'wide')
- thermal_distributions_after: float32 [7, 512, 128, 128], P(None, 'narrow', 'wide')
- cube_warmth_values: float32 [1024, 16, 256], P(('narrow', 'wide'))
The draws below stay inside these ranges and needn't reach their ends.
Inputs may be any that keep to these rules, and one draw needn't show every extreme that they name: `owner_of`: among one device's 256 rows, each owner is named at most 16 times, and in some device's rows some owner is named exactly 16 times. `flow_state`: populations are positive. `thermal_distributions_current`: populations are positive.
All inputs are finite; a program needn't handle non-finite values. No bound on the sum of `fluid_mask` on one device may be relied on, other than what follows from the above.
Results may differ from the reference program's by a relative error of at most 0.000075.
Values sent between devices are 32-bit elements; how exact they have to be, the bound alone decides.
No kernel may reach another device: no remote copies, remote signals or barrier semaphores. Data moves between devices by JAX's collectives and lax.ppermute only.
A program may use at most 32 MiB of HBM per device.

```python
import math
import jax
import jax.numpy as jnp
import numpy as np
from jax import lax

BX = 8
BY = 8
NZ = 128
CUBE_SPAN_POINTS = 16
SB = 1
IR = 256
CAP = 16
NX = 512
NY = 128
SOLID_CUBES = 1024
ROWS_ALL = 262144
N_NARROW = 64
N_WIDE = 16


draw_velocity = np.array([[0, 0, 0], [1, 0, 0], [-1, 0, 0], [0, 1, 0], [0, -1, 0], [0, 0, 1], [0, 0, -1], [1, 1, 0], [-1, -1, 0], [1, -1, 0], [-1, 1, 0], [1, 0, 1], [-1, 0, -1], [1, 0, -1], [-1, 0, 1], [0, 1, 1], [0, -1, -1], [0, 1, -1], [0, -1, 1]], dtype=np.int32)


draw_flow_weight = [1.0 / 3.0] + [1.0 / 18.0] * 6 + [1.0 / 36.0] * 12


draw_thermal_stencil_coefficient = [0.25] + [0.125] * 6


def draw_flow_state(key, part):
    key = jax.random.fold_in(key, 11)
    subkeys = jax.random.split(key, 3)
    grid_shape = (NX, NY, NZ)
    density = 1.0 + 0.1 * jax.random.uniform(subkeys[0], grid_shape, jnp.float32, -1.0, 1.0)
    velocity = jax.random.uniform(subkeys[1], (3, NX, NY, NZ), jnp.float32, -0.05, 0.05)
    square = velocity[0] * velocity[0] + velocity[1] * velocity[1] + velocity[2] * velocity[2]
    jitter = 1.0 + 0.2 * jax.random.uniform(subkeys[2], (19, NX, NY, NZ), jnp.float32, -1.0, 1.0)
    flow_parts = []
    for speed_coordinate in range(19):
        direction = draw_velocity[speed_coordinate]
        directional_speed_product = float(direction[0]) * velocity[0] + float(direction[1]) * velocity[1] + float(direction[2]) * velocity[2]
        balanced_distribution = draw_flow_weight[speed_coordinate] * density * (1.0 + 3.0 * directional_speed_product + 4.5 * directional_speed_product * directional_speed_product - 1.5 * square)
        flow_parts.append(balanced_distribution * jitter[speed_coordinate])
    return jnp.stack(flow_parts)


def draw_thermal_distributions_current(key, part):
    key = jax.random.fold_in(key, 23)
    subkeys = jax.random.split(key, 2)
    grid_shape = (NX, NY, NZ)
    theta = 0.5 + 1.5 * jax.random.uniform(subkeys[0], grid_shape, jnp.float32, 0.0, 1.0)
    jitter = 1.0 + 0.2 * jax.random.uniform(subkeys[1], (7, NX, NY, NZ), jnp.float32, -1.0, 1.0)
    heat_parts = [draw_thermal_stencil_coefficient[speed_coordinate] * theta * jitter[speed_coordinate] for speed_coordinate in range(7)]
    return jnp.stack(heat_parts)


def with_ends(result, rng, smallest, top_value):
    shape = result.shape
    place = [jax.random.randint(jax.random.fold_in(rng, axis), (), 0, shape[axis]) for axis in range(len(shape))]
    result = result.at[tuple(place)].set(smallest)
    longest = shape.index(max(shape))
    place[longest] = (place[longest] + 1) % shape[longest]
    return result.at[tuple(place)].set(top_value)


def block_scale(own_key, shape, shards, low, top_value):
    gain, own = 1.0, jax.random.fold_in(own_key, 6)
    for position, shards_of in shards:
        heights = jnp.exp(jax.random.uniform(jax.random.fold_in(own, position), (shards_of,), jnp.float32, low / len(shards), top_value / len(shards)))
        gain = gain * jnp.repeat(heights, shape[position] // shards_of).reshape([-1 if axis == position else 1 for axis in range(len(shape))])
    return gain


def routed_block(key, own, number, rows, count, top, reach, skew):
    ranking = jax.random.permutation(key, count)
    crowded, usual = portions_of(count, rows * top, reach, skew, True), portions_of(count, rows * top, reach, skew, False)
    places = jnp.arange(count)

    def named(lengths, offset_by):
        used = int((lengths > 0).sum())
        fixed = max(1, used // 4)
        shifted = fixed + (places - fixed + offset_by * (used - fixed)) % max(1, count - fixed)
        return jnp.zeros((count,), jnp.int32).at[ranking[jnp.where(places < fixed, places, shifted)]].set(jnp.asarray(lengths, jnp.int32))

    lengths = jnp.where(number % 4 == 0, named(crowded, number // 4), named(usual, number - number // 4 - 1))
    mixed = jax.random.permutation(jax.random.fold_in(own, 3), count)
    donor, receiver = mixed[0:count // 2 * 2:2], mixed[1:count // 2 * 2:2]
    slack = jnp.minimum(lengths[donor] - 1, reach - lengths[receiver]) // 2
    slack = jnp.where((donor == ranking[0]) | (receiver == ranking[0]) | (lengths[receiver] == 0), 0, jnp.maximum(slack, 0))
    shifted = jax.random.randint(jax.random.fold_in(own, 4), (count // 2,), 0, 1 << 20) % (slack + 1)
    lengths = lengths.at[donor].add(-shifted).at[receiver].add(shifted)
    labels = jnp.searchsorted(jnp.cumsum(lengths), jnp.arange(rows * top), side="right").astype(jnp.int32)
    listing = labels.reshape(top, rows).T
    listing = listing[jax.random.permutation(jax.random.fold_in(own, 1), rows)]
    offset_by = jax.random.randint(jax.random.fold_in(own, 2), (rows, 1), 0, top)
    return jnp.take_along_axis(listing, (jnp.arange(top)[None, :] + offset_by) % top, axis=1)


def portions_of(count, total, reach, skew, full):
    portions = [(1 << 20) // math.isqrt(standing ** skew) + 1 for standing in range(1, count + 1)]
    largest = reach if full else min(reach, max(-(-total // count), total * portions[0] // sum(portions)))
    least = 1 if total - largest >= count - 1 else 0
    given, spare = [largest] + [least] * (count - 1), total - largest - least * (count - 1)
    while spare > 0:
        candidates = [i for i in range(1, count) if given[i] < largest] or [i for i in range(1, count) if given[i] < reach]
        pool, budget = sum([portions[i] for i in candidates]), spare
        for i in candidates:
            more = min(reach - given[i], max(1, budget * portions[i] // pool), spare)
            given[i] = given[i] + more
            spare = spare - more
    return np.array(given)


def bell_draw(own_key, dims, width, reach, cuts=(), kind=jnp.bfloat16):
    entries = width * jax.random.normal(own_key, dims, jnp.float32)
    if cuts:
        entries = entries * block_scale(own_key, dims, cuts, -0.22, 0.18)
    return jnp.clip(entries, -reach, reach).astype(kind)


def setup_inputs(seed: int = 0) -> dict:
    arg_keys = jax.random.split(jax.random.key(seed), 10)
    flow_state = draw_flow_state(jax.random.fold_in(arg_keys[9], 71), 0)
    thermal_distributions_current = draw_thermal_distributions_current(jax.random.fold_in(arg_keys[9], 71), 0)
    fluid_mask = with_ends((jax.random.randint(arg_keys[2], (NX, NY, NZ), 0, 10) < 7).astype(jnp.int32), jax.random.fold_in(arg_keys[2], 1), 0, 1)
    heat_rate = jnp.clip(jnp.exp(math.log(1.8) - 1.0986122 * jax.random.uniform(arg_keys[3], (NX, NY, NZ), jnp.float32) ** block_scale(arg_keys[3], (NX, NY, NZ), ((0, 64), (1, 16)), -0.2, 0.2)), 0.6, 1.8)
    solid_source = bell_draw(arg_keys[4], (SOLID_CUBES, CUBE_SPAN_POINTS, CUBE_SPAN_POINTS * CUBE_SPAN_POINTS), 1.0, 6.0, ((0, 1024),), jnp.float32)
    cube_uptake_coefficients = jnp.clip(jnp.exp(math.log(0.5) - 2.3025851 * jax.random.uniform(arg_keys[5], (SOLID_CUBES,), jnp.float32) ** block_scale(arg_keys[5], (SOLID_CUBES,), ((0, 1024),), -0.2, 0.2)), 0.05, 0.5)
    owner_of_keys = jax.random.split(jax.random.fold_in(arg_keys[6], 1), ROWS_ALL // IR)
    owner_of_turns = jax.random.permutation(jax.random.fold_in(arg_keys[6], 3), ROWS_ALL // IR)
    owner_of = jax.vmap(lambda own, number: routed_block(jax.random.fold_in(arg_keys[6], 2), own, number, IR, N_NARROW, 1, CAP, 2))(owner_of_keys, owner_of_turns).reshape((ROWS_ALL, 1))
    emitting_grid_site = with_ends(jax.random.randint(arg_keys[7], (ROWS_ALL,), 0, BX * BY * NZ), jax.random.fold_in(arg_keys[7], 1), 0, (BX * BY * NZ) - 1).astype(jnp.int32)
    target_node = with_ends(jax.random.randint(arg_keys[8], (ROWS_ALL,), 0, SB * CUBE_SPAN_POINTS * CUBE_SPAN_POINTS), jax.random.fold_in(arg_keys[8], 1), 0, (SB * CUBE_SPAN_POINTS * CUBE_SPAN_POINTS) - 1).astype(jnp.int32)
    return {"flow_state": flow_state, "thermal_distributions_current": thermal_distributions_current, "fluid_mask": fluid_mask, "heat_rate": heat_rate, "solid_source": solid_source, "cube_uptake_coefficients": cube_uptake_coefficients, "owner_of": owner_of, "emitting_grid_site": emitting_grid_site, "target_node": target_node}


flow_velocity = np.array([[0, 0, 0], [1, 0, 0], [-1, 0, 0], [0, 1, 0], [0, -1, 0], [0, 0, 1], [0, 0, -1], [1, 1, 0], [-1, -1, 0], [1, -1, 0], [-1, 1, 0], [1, 0, 1], [-1, 0, -1], [1, 0, -1], [-1, 0, 1], [0, 1, 1], [0, -1, -1], [0, 1, -1], [0, -1, 1]], dtype=np.int32)
flow_opposite = [0, 2, 1, 4, 3, 6, 5, 8, 7, 10, 9, 12, 11, 14, 13, 16, 15, 18, 17]
flow_weight = [1.0 / 3.0] + [1.0 / 18.0] * 6 + [1.0 / 36.0] * 12
thermal_stencil_coefficient = [0.25] + [0.125] * 6
flow_rate = 1.2
interface_exchange = 0.5

def moment(stacked, axis_number):
    running = jnp.zeros_like(stacked[0])
    for speed_coordinate in range(stacked.shape[0]):
        direction = int(flow_velocity[speed_coordinate, axis_number])
        if direction > 0:
            running = running + stacked[speed_coordinate]
        elif direction < 0:
            running = running - stacked[speed_coordinate]
    return running

def collide(flow_state, thermal_distributions_current, fluid_mask, heat_rate):
    density = lax.optimization_barrier(jnp.sum(flow_state, axis=0))
    speed_x = moment(flow_state, 0) / density
    speed_y = moment(flow_state, 1) / density
    speed_z = moment(flow_state, 2) / density
    square = speed_x * speed_x + speed_y * speed_y + speed_z * speed_z
    is_fluid = fluid_mask == 1
    flow_parts = []
    for speed_coordinate in range(19):
        velocity = flow_velocity[speed_coordinate]
        directional_speed_product = float(velocity[0]) * speed_x + float(velocity[1]) * speed_y + float(velocity[2]) * speed_z
        balanced_distribution = flow_weight[speed_coordinate] * density * (1.0 + 3.0 * directional_speed_product + 4.5 * directional_speed_product * directional_speed_product - 1.5 * square)
        relaxed = flow_state[speed_coordinate] - flow_rate * (flow_state[speed_coordinate] - balanced_distribution)
        flow_parts.append(jnp.where(is_fluid, relaxed, flow_state[flow_opposite[speed_coordinate]]))
    coolant_warmth = lax.optimization_barrier(jnp.sum(thermal_distributions_current, axis=0))
    heat_parts = []
    for speed_coordinate in range(7):
        velocity = flow_velocity[speed_coordinate]
        directional_speed_product = float(velocity[0]) * speed_x + float(velocity[1]) * speed_y + float(velocity[2]) * speed_z
        balanced_distribution = thermal_stencil_coefficient[speed_coordinate] * coolant_warmth * (1.0 + 4.0 * directional_speed_product)
        relaxed = thermal_distributions_current[speed_coordinate] - heat_rate * (thermal_distributions_current[speed_coordinate] - balanced_distribution)
        heat_parts.append(jnp.where(is_fluid, relaxed, thermal_distributions_current[flow_opposite[speed_coordinate]]))
    return (flow_parts, heat_parts)

def sine_table(size):
    counting = jnp.arange(1, size + 1, dtype=jnp.float32)
    angles = math.pi * counting[:, None] * counting[None, :] / (size + 1)
    eigen_vectors = math.sqrt(2.0 / (size + 1)) * jnp.sin(angles)
    eigen_values = 2.0 - 2.0 * jnp.cos(math.pi * counting / (size + 1))
    return (eigen_vectors, eigen_values)

def compute_cube_diffusion(system_load_vector, cube_uptake_coefficients, size):
    eigen_vectors, eigen_values = sine_table(size)
    blocks = system_load_vector.shape[0]
    block_cube = system_load_vector.reshape(blocks, size, size, size)
    highest = lax.Precision.HIGHEST
    spectral = jnp.einsum('ai,bijk->bajk', eigen_vectors, block_cube, precision=highest)
    spectral = jnp.einsum('aj,bijk->biak', eigen_vectors, spectral, precision=highest)
    spectral = jnp.einsum('ak,bijk->bija', eigen_vectors, spectral, precision=highest)
    denominator = cube_uptake_coefficients[:, None, None, None] + eigen_values[None, :, None, None] + eigen_values[None, None, :, None] + eigen_values[None, None, None, :]
    spectral = spectral / denominator
    spectral = jnp.einsum('ai,bijk->bajk', eigen_vectors, spectral, precision=highest)
    spectral = jnp.einsum('aj,bijk->biak', eigen_vectors, spectral, precision=highest)
    spectral = jnp.einsum('ak,bijk->bija', eigen_vectors, spectral, precision=highest)
    return spectral.reshape(blocks, size, size * size)

def stream_global(plane, speed_coordinate):
    velocity = flow_velocity[speed_coordinate]
    return jnp.roll(plane, (int(velocity[0]), int(velocity[1]), int(velocity[2])), axis=(0, 1, 2))

def reference(flow_state, thermal_distributions_current, fluid_mask, heat_rate, solid_source, cube_uptake_coefficients, owner_of, emitting_grid_site, target_node):
    flow_parts, heat_parts = collide(flow_state, thermal_distributions_current, fluid_mask, heat_rate)
    stream_distributions_after = jnp.stack([stream_global(flow_parts[speed_coordinate], speed_coordinate) for speed_coordinate in range(19)])
    moved_distributions = [stream_global(heat_parts[speed_coordinate], speed_coordinate) for speed_coordinate in range(7)]
    coolant_warmth = lax.optimization_barrier(jnp.sum(jnp.stack(moved_distributions), axis=0))
    row_ids = jnp.arange(ROWS_ALL, dtype=jnp.int32)
    device = row_ids // IR
    row_narrow = device // N_WIDE
    row_wide = device % N_WIDE
    local_x = emitting_grid_site // (BY * NZ)
    local_y = emitting_grid_site // NZ % BY
    brick_vertical_offset = emitting_grid_site % NZ
    whole_domain_abscissa = row_narrow * BX + local_x
    whole_domain_ordinate = row_wide * BY + local_y
    interface_entry_warmth = coolant_warmth[whole_domain_abscissa, whole_domain_ordinate, brick_vertical_offset]
    owners = owner_of[:, 0]
    facet_number = (owners * N_WIDE + row_wide) * (SB * CUBE_SPAN_POINTS * CUBE_SPAN_POINTS) + target_node
    facet_heating = jax.ops.segment_sum(interface_exchange * interface_entry_warmth, facet_number, num_segments=SOLID_CUBES * CUBE_SPAN_POINTS * CUBE_SPAN_POINTS)
    system_load_vector = solid_source.at[:, 0, :].add(facet_heating.reshape(SOLID_CUBES, CUBE_SPAN_POINTS * CUBE_SPAN_POINTS))
    cube_warmth_values = compute_cube_diffusion(system_load_vector, cube_uptake_coefficients, CUBE_SPAN_POINTS)
    boundary_sites = cube_warmth_values[:, 0, :].reshape(-1)
    interface_entry_flux = interface_exchange * (boundary_sites[facet_number] - interface_entry_warmth)
    cell_index = (whole_domain_abscissa * NY + whole_domain_ordinate) * NZ + brick_vertical_offset
    heat_gain = jax.ops.segment_sum(interface_entry_flux, cell_index, num_segments=NX * NY * NZ).reshape(NX, NY, NZ)
    thermal_distributions_after = jnp.stack([moved_distributions[speed_coordinate] + thermal_stencil_coefficient[speed_coordinate] * heat_gain for speed_coordinate in range(7)])
    return (stream_distributions_after, thermal_distributions_after, cube_warmth_values)
```

```python
import functools
import math

import jax
import jax.numpy as jnp
import numpy as np
from jax import lax
from jax.experimental import pallas as pl
from jax.experimental.pallas import tpu as pltpu
from jax.sharding import PartitionSpec as P

flow_velocity = np.array(
    [
        [0, 0, 0],
        [1, 0, 0],
        [-1, 0, 0],
        [0, 1, 0],
        [0, -1, 0],
        [0, 0, 1],
        [0, 0, -1],
        [1, 1, 0],
        [-1, -1, 0],
        [1, -1, 0],
        [-1, 1, 0],
        [1, 0, 1],
        [-1, 0, -1],
        [1, 0, -1],
        [-1, 0, 1],
        [0, 1, 1],
        [0, -1, -1],
        [0, 1, -1],
        [0, -1, 1],
    ],
    dtype=np.int32,
)
flow_opposite = [0, 2, 1, 4, 3, 6, 5, 8, 7, 10, 9, 12, 11, 14, 13, 16, 15, 18, 17]
flow_weight = [1.0 / 3.0] + [1.0 / 18.0] * 6 + [1.0 / 36.0] * 12
thermal_stencil_coefficient = [0.25] + [0.125] * 6
flow_rate = 1.2
interface_exchange = 0.5

x_up = (1, 7, 9, 11, 13)
x_down = (2, 8, 10, 12, 14)
y_up = (3, 15, 17)
y_down = (4, 16, 18)
diagonal_up = (7, 10)
diagonal_down = (8, 9)

HIGHEST = lax.Precision.HIGHEST
params = pltpu.CompilerParams(vmem_limit_bytes=32 * 1024 * 1024)


def sine_constants(size):
    counting = np.arange(1, size + 1, dtype=np.float64)
    sine = math.sqrt(2.0 / (size + 1)) * np.sin(
        math.pi * counting[:, None] * counting[None, :] / (size + 1)
    )
    values = 2.0 - 2.0 * np.cos(math.pi * counting / (size + 1))
    plane = np.kron(sine, sine)
    total = values[:, None] + (values[:, None] + values[None, :]).reshape(1, -1)
    return (
        sine.astype(np.float32),
        plane.astype(np.float32),
        total.astype(np.float32),
        np.ascontiguousarray(np.broadcast_to(sine[:, :1], total.shape)).astype(np.float32),
    )


def dot(a, b, precision=None):
    return lax.dot_general(
        a, b, (((1,), (0,)), ((), ())), precision=precision, preferred_element_type=jnp.float32
    )


def dot_last(a, b):
    return lax.dot_general(a, b, (((1,), (1,)), ((), ())), preferred_element_type=jnp.float32)


def parts_of(value, count):
    parts = []
    for _ in range(count):
        part = value.astype(jnp.bfloat16)
        parts.append(part)
        value = value - part.astype(jnp.float32)
    return parts


def one_hot(row, size):
    numbers = lax.broadcasted_iota(jnp.int32, (size, row.shape[1]), 0)
    return jnp.where(numbers == row, 1.0, 0.0).astype(jnp.bfloat16)


def collide_kernel(
    flow_ref, heat_ref, mask_ref, rate_ref,
    post_ref, heat_post_ref, xu_ref, xd_ref, yu_ref, yd_ref, du_ref, dd_ref,
):
    wide_x, wide_y = flow_ref.shape[1], flow_ref.shape[2]
    for x in range(wide_x):
        f = [flow_ref[i, x] for i in range(19)]
        density = functools.reduce(lambda a, b: a + b, f)
        momentum = []
        for axis in range(3):
            plus = [f[i] for i in range(19) if flow_velocity[i, axis] > 0]
            minus = [f[i] for i in range(19) if flow_velocity[i, axis] < 0]
            momentum.append(
                functools.reduce(lambda a, b: a + b, plus)
                - functools.reduce(lambda a, b: a + b, minus)
            )
        inverse = 1.0 / density
        speed = [m * inverse for m in momentum]
        square = speed[0] * speed[0] + speed[1] * speed[1] + speed[2] * speed[2]
        base = 1.0 - 1.5 * square
        is_fluid = mask_ref[x] == 1

        def along(i):
            total = None
            for axis in range(3):
                c = int(flow_velocity[i, axis])
                if c == 0:
                    continue
                term = speed[axis] if c > 0 else -speed[axis]
                total = term if total is None else total + term
            return total

        weighted = {w: density * w for w in set(flow_weight)}
        post = [None] * 19
        for i in [0] + list(range(1, 19, 2)):
            scale = weighted[flow_weight[i]]
            if i == 0:
                post[0] = jnp.where(is_fluid, f[0] - flow_rate * (f[0] - scale * base), f[0])
                continue
            cu = along(i)
            even = base + 4.5 * (cu * cu)
            odd = 3.0 * cu
            for k, balanced in ((i, scale * (even + odd)), (i + 1, scale * (even - odd))):
                post[k] = jnp.where(
                    is_fluid, f[k] - flow_rate * (f[k] - balanced), f[flow_opposite[k]]
                )
        h = [heat_ref[i, x] for i in range(7)]
        warmth = functools.reduce(lambda a, b: a + b, h)
        rate = rate_ref[x]
        heat = []
        for i in range(7):
            scale = thermal_stencil_coefficient[i] * warmth
            balanced = scale if i == 0 else scale * (1.0 + 4.0 * along(i))
            heat.append(jnp.where(is_fluid, h[i] - rate * (h[i] - balanced), h[flow_opposite[i]]))
        for i in range(19):
            post_ref[i, x] = post[i]
        for i in range(7):
            heat_post_ref[i, x] = heat[i]
        if x == wide_x - 1:
            for slot, part in enumerate([heat[1]] + [post[i] for i in x_up]):
                xu_ref[slot] = part
        if x == 0:
            for slot, part in enumerate([heat[2]] + [post[i] for i in x_down]):
                xd_ref[slot] = part
        last, row = slice(wide_y - 1, wide_y), slice(x, x + 1)
        for slot, part in enumerate([heat[3]] + [post[i] for i in y_up]):
            yu_ref[slot, row, :] = part[last]
        for slot, part in enumerate([heat[4]] + [post[i] for i in y_down]):
            yd_ref[slot, row, :] = part[0:1]
        for slot, i in enumerate(diagonal_up):
            du_ref[slot, row, :] = post[i][last]
        for slot, i in enumerate(diagonal_down):
            dd_ref[slot, row, :] = post[i][0:1]


def block_kernel(
    source_ref, uptake_ref, sine_ref, plane_ref, total_ref, first_ref, cube_ref, reply_ref
):
    sine, plane = sine_ref[...], plane_ref[...]
    inverse = 1.0 / (total_ref[...] + uptake_ref[0])
    spectral = dot(dot(sine, source_ref[0], HIGHEST), plane, HIGHEST) * inverse
    cube_ref[...] = dot(dot(sine, spectral, HIGHEST), plane, HIGHEST)
    reply_ref[...] = dot(sine, first_ref[...] * inverse, HIGHEST)


def shifted_y(value, direction, edge):
    size = value.shape[0]
    rows = lax.broadcasted_iota(jnp.int32, value.shape, 0)
    if direction > 0:
        return jnp.where(rows == 0, edge, pltpu.roll(value, 1, 0))
    return jnp.where(rows == size - 1, edge, pltpu.roll(value, size - 1, 0))


def shifted_z(value, direction):
    if direction == 0:
        return value
    return pltpu.roll(value, 1 if direction > 0 else value.shape[1] - 1, 1)


def site_one_hots(site_ref, planes, depth):
    rows = site_ref[...]
    row = jnp.concatenate([rows[0:1], rows[1:2]], axis=1)
    return one_hot(row // depth, planes), one_hot(row % depth, depth)


def warmth_kernel(
    heat_post_ref, xu_ref, xd_ref, yu_ref, yd_ref, du_ref, dd_ref,
    site_ref, owner_ref, node_ref, wide_ref, cube_ref, reply_ref,
    passed_ref, warmth_ref, send_ref, du_out_ref, dd_out_ref, *, n_wide, face,
):
    wide_x, wide_y, depth = heat_post_ref.shape[1:]
    planes = []
    for x in range(wide_x):
        passed = [
            heat_post_ref[0, x],
            xu_ref[0] if x == 0 else heat_post_ref[1, x - 1],
            xd_ref[0] if x == wide_x - 1 else heat_post_ref[2, x + 1],
            shifted_y(heat_post_ref[3, x], 1, yu_ref[0, x : x + 1, :]),
            shifted_y(heat_post_ref[4, x], -1, yd_ref[0, x : x + 1, :]),
            shifted_z(heat_post_ref[5, x], 1),
            shifted_z(heat_post_ref[6, x], -1),
        ]
        for i in range(7):
            passed_ref[i, x] = passed[i]
        planes.append(functools.reduce(lambda a, b: a + b, passed))
    field = jnp.concatenate(planes, axis=0)
    count = wide_x * wide_y
    at_plane, at_depth = site_one_hots(site_ref, count, depth)
    picked = dot(jnp.concatenate(parts_of(field, 3), axis=0), at_depth)
    picked = picked[0:count] + picked[count : 2 * count] + picked[2 * count :]
    warmth = jnp.sum(picked * at_plane.astype(jnp.float32), axis=0, keepdims=True)
    warmth_ref[...] = warmth
    number = ((owner_ref[...] * n_wide + wide_ref[0]) * face + node_ref[...]).astype(jnp.float32)
    half = face // 2
    message = jnp.concatenate(
        [
            warmth[:, 0:half], warmth[:, half:], number,
            cube_ref[0:1, 0:half], cube_ref[0:1, half:],
            reply_ref[0:1, 0:half], reply_ref[0:1, half:],
        ],
        axis=0,
    )
    for peer in range(send_ref.shape[0]):
        send_ref[peer] = message
    for slot, i in enumerate(diagonal_up):
        rows = lax.broadcasted_iota(jnp.int32, (wide_x, depth), 0)
        if flow_velocity[i, 0] > 0:
            edge = xu_ref[1 + x_up.index(i), wide_y - 1 : wide_y, :]
            du_out_ref[slot] = jnp.where(rows == 0, edge, pltpu.roll(du_ref[slot], 1, 0))
        else:
            edge = xd_ref[1 + x_down.index(i), wide_y - 1 : wide_y, :]
            du_out_ref[slot] = jnp.where(
                rows == wide_x - 1, edge, pltpu.roll(du_ref[slot], wide_x - 1, 0)
            )
    for slot, i in enumerate(diagonal_down):
        rows = lax.broadcasted_iota(jnp.int32, (wide_x, depth), 0)
        if flow_velocity[i, 0] > 0:
            edge = xu_ref[1 + x_up.index(i), 0:1, :]
            dd_out_ref[slot] = jnp.where(rows == 0, edge, pltpu.roll(dd_ref[slot], 1, 0))
        else:
            edge = xd_ref[1 + x_down.index(i), 0:1, :]
            dd_out_ref[slot] = jnp.where(
                rows == wide_x - 1, edge, pltpu.roll(dd_ref[slot], wide_x - 1, 0)
            )


def stream_kernel(post_ref, xu_ref, xd_ref, yu_ref, yd_ref, du_ref, dd_ref, out_ref):
    wide_x = post_ref.shape[1]
    for i in range(19):
        cx, cy, cz = (int(c) for c in flow_velocity[i])
        for x in range(wide_x):
            if cx > 0 and x == 0:
                value = xu_ref[1 + x_up.index(i)]
            elif cx < 0 and x == wide_x - 1:
                value = xd_ref[1 + x_down.index(i)]
            else:
                value = post_ref[i, x - cx]
            if cy:
                if cx:
                    edges = du_ref if cy > 0 else dd_ref
                    slot = (diagonal_up if cy > 0 else diagonal_down).index(i)
                else:
                    edges = yu_ref if cy > 0 else yd_ref
                    slot = 1 + (y_up if cy > 0 else y_down).index(i)
                value = shifted_y(value, cy, edges[slot, x : x + 1, :])
            out_ref[i, x] = shifted_z(value, cz)


def finish_kernel(
    got_ref, passed_ref, warmth_ref, site_ref, owner_ref, node_ref, me_ref, cube_ref, reply_ref,
    plane_ref, heat_ref, cube_out_ref, high_ref, low_ref, owner_rows_ref, node_rows_ref, table_ref,
    *, n_wide, face,
):
    peers, depth = got_ref.shape[0] // 8, got_ref.shape[1]
    wide_x, wide_y = passed_ref.shape[1:3]
    bits = lambda row: got_ref[pl.ds(row, peers, stride=8), :]
    for half in range(2):
        temperature = bits(half)
        high = temperature.astype(jnp.bfloat16).astype(jnp.float32)
        high_ref[half] = high
        low_ref[half] = temperature - high
        number = bits(2 + half).astype(jnp.int32)
        owner_rows_ref[half] = (number // (n_wide * face)).astype(jnp.float32)
        node_rows_ref[half] = (number % face).astype(jnp.float32)

    def spread(ref, half, d):
        row = ref[half, pl.ds(d, 1), :]
        return jnp.broadcast_to(row, (16, depth)).astype(jnp.bfloat16)

    numbers = lax.broadcasted_iota(jnp.int32, (16, depth), 0).astype(jnp.float32)
    zero = jnp.zeros((16, depth), jnp.bfloat16)
    one = jnp.ones((16, depth), jnp.bfloat16)
    owner_groups = -(-peers // 16)

    def step(block, total):
        left, right = [], []
        for inner in range(unroll):
            d = block * unroll + inner
            for half in range(2):
                node, owner = spread(node_rows_ref, half, d), spread(owner_rows_ref, half, d)
                high, low = spread(high_ref, half, d), spread(low_ref, half, d)
                wanted = [(numbers + 16.0 * g).astype(jnp.bfloat16) for g in range(face // 16)]
                right.append(
                    jnp.concatenate([jnp.where(node == w, one, zero) for w in wanted], axis=0)
                )
                hits = [owner == wanted[g] for g in range(owner_groups)]
                left.append(
                    jnp.concatenate(
                        [jnp.where(hit, high, zero) for hit in hits]
                        + [jnp.where(hit, low, zero) for hit in hits],
                        axis=0,
                    )
                )
        return total + dot_last(
            jnp.concatenate(left, axis=1), jnp.concatenate(right, axis=1)
        )

    unroll = math.gcd(peers, 8)
    both = lax.fori_loop(
        0, peers // unroll, step, jnp.zeros((2 * 16 * owner_groups, face), jnp.float32)
    )
    table = interface_exchange * (both[0:peers] + both[16 * owner_groups :][0:peers])
    plane = plane_ref[...]
    spectral = dot(table, plane, HIGHEST)
    table_ref[...] = spectral
    reply = jnp.concatenate([bits(6), bits(7)], axis=1)
    own = table_ref[pl.ds(me_ref[0], 1), :]
    answers = dot(
        jnp.concatenate([spectral * reply, reply_ref[...] * own], axis=0), plane, HIGHEST
    )
    surface = answers[0:peers] + jnp.concatenate([bits(4), bits(5)], axis=1)
    cube_out_ref[0] = cube_ref[...] + answers[peers:]

    owners, nodes = owner_ref[...], node_ref[...]
    at_owner = one_hot(jnp.concatenate([owners[0:1], owners[1:2]], axis=1), peers)
    at_node = one_hot(jnp.concatenate([nodes[0:1], nodes[1:2]], axis=1), face)
    picked = dot(jnp.concatenate(parts_of(surface, 3), axis=0), at_node)
    picked = picked[0:peers] + picked[peers : 2 * peers] + picked[2 * peers :]
    boundary = jnp.sum(picked * at_owner.astype(jnp.float32), axis=0, keepdims=True)
    flux = interface_exchange * (boundary - warmth_ref[...])
    count = wide_x * wide_y
    at_plane, at_depth = site_one_hots(site_ref, count, depth)
    flux_parts = [
        at_plane * jnp.broadcast_to(part, at_plane.shape) for part in parts_of(flux, 3)
    ]
    gain = dot_last(jnp.concatenate(flux_parts, axis=0), at_depth)
    gain = gain[0:count] + gain[count : 2 * count] + gain[2 * count :]
    for x in range(wide_x):
        rows = gain[x * wide_y : (x + 1) * wide_y]
        for i in range(7):
            heat_ref[i, x] = passed_ref[i, x] + thermal_stencil_coefficient[i] * rows


def call(kernel, shapes, *operands, smem=(), scratch=(), cost=1000000):
    specs = [
        pl.BlockSpec(memory_space=pltpu.SMEM if i in smem else pltpu.VMEM)
        for i in range(len(operands))
    ]
    out_specs = [pl.BlockSpec(memory_space=pltpu.VMEM) for _ in shapes]
    moved = sum(4 * math.prod(o.shape) for o in list(operands) + list(shapes))
    return pl.pallas_call(
        kernel,
        out_shape=list(shapes),
        in_specs=specs,
        out_specs=out_specs,
        scratch_shapes=list(scratch),
        compiler_params=params,
        cost_estimate=pl.CostEstimate(flops=cost, bytes_accessed=moved, transcendentals=0),
    )(*operands)


def f32(*shape):
    return jax.ShapeDtypeStruct(shape, jnp.float32)


def per_device(
    flow_state,
    thermal_distributions_current,
    fluid_mask,
    heat_rate,
    solid_source,
    cube_uptake_coefficients,
    owner_of,
    emitting_grid_site,
    target_node,
):
    bx, by, nz = fluid_mask.shape
    size, face = solid_source.shape[1:]
    peers, n_wide = lax.axis_size("narrow"), lax.axis_size("wide")
    rows = emitting_grid_site.shape[0]
    site = emitting_grid_site.reshape(2, rows // 2)
    owner = owner_of.reshape(2, rows // 2)
    node = target_node.reshape(2, rows // 2)
    me = lax.axis_index("narrow").astype(jnp.int32).reshape(1)
    wide = lax.axis_index("wide").astype(jnp.int32).reshape(1)
    sine, plane, total, first = (jnp.asarray(c) for c in sine_constants(size))

    post, heat_post, xu, xd, yu, yd, du, dd = call(
        collide_kernel,
        (
            f32(19, bx, by, nz), f32(7, bx, by, nz), f32(6, by, nz), f32(6, by, nz),
            f32(4, bx, nz), f32(4, bx, nz), f32(2, bx, nz), f32(2, bx, nz),
        ),
        flow_state, thermal_distributions_current, fluid_mask, heat_rate,
    )
    cube, reply = call(
        block_kernel,
        (f32(size, face), f32(size, face)),
        solid_source, cube_uptake_coefficients, sine, plane, total, first,
        smem=(1,),
    )

    def send(block, axis, step):
        count = lax.axis_size(axis)
        return lax.ppermute(block, axis, [(i, (i + step) % count) for i in range(count)])

    xu, xd = send(xu, "narrow", 1), send(xd, "narrow", -1)
    yu, yd = send(yu, "wide", 1), send(yd, "wide", -1)
    passed, warmth, message, du, dd = call(
        functools.partial(warmth_kernel, n_wide=n_wide, face=face),
        (
            f32(7, bx, by, nz), f32(1, rows), f32(peers, 8, face // 2),
            f32(2, bx, nz), f32(2, bx, nz),
        ),
        heat_post, xu, xd, yu, yd, du, dd, site, owner, node, wide, cube, reply,
        smem=(10,),
    )
    got = lax.all_to_all(message, "narrow", split_axis=0, concat_axis=0, tiled=True)
    du, dd = send(du, "wide", 1), send(dd, "wide", -1)
    (stream,) = call(
        stream_kernel, (f32(19, bx, by, nz),), post, xu, xd, yu, yd, du, dd
    )
    heat, cubes = call(
        functools.partial(finish_kernel, n_wide=n_wide, face=face),
        (f32(7, bx, by, nz), f32(1, size, face)),
        got.reshape(peers * 8, face // 2), passed, warmth, site, owner, node, me, cube, reply,
        plane,
        smem=(6,),
        scratch=[pltpu.VMEM((2, peers, face // 2), jnp.float32)] * 4
        + [pltpu.VMEM((peers, face), jnp.float32)],
    )
    return stream, heat, cubes


def solution(mesh):
    return jax.shard_map(
        per_device,
        mesh=mesh,
        in_specs=(
            P(None, "narrow", "wide", None),
            P(None, "narrow", "wide", None),
            P("narrow", "wide", None),
            P("narrow", "wide", None),
            P(("narrow", "wide"), None, None),
            P(("narrow", "wide")),
            P(("narrow", "wide"), None),
            P(("narrow", "wide")),
            P(("narrow", "wide")),
        ),
        out_specs=(
            P(None, "narrow", "wide", None),
            P(None, "narrow", "wide", None),
            P(("narrow", "wide"), None, None),
        ),
        check_vma=False,
    )
```

```python
import functools
import math

import jax
import jax.numpy as jnp
import numpy as np
from jax import lax
from jax.experimental import pallas as pl
from jax.experimental.pallas import tpu as pltpu
from jax.sharding import PartitionSpec as P

flow_velocity = np.array(
    [
        [0, 0, 0],
        [1, 0, 0],
        [-1, 0, 0],
        [0, 1, 0],
        [0, -1, 0],
        [0, 0, 1],
        [0, 0, -1],
        [1, 1, 0],
        [-1, -1, 0],
        [1, -1, 0],
        [-1, 1, 0],
        [1, 0, 1],
        [-1, 0, -1],
        [1, 0, -1],
        [-1, 0, 1],
        [0, 1, 1],
        [0, -1, -1],
        [0, 1, -1],
        [0, -1, 1],
    ],
    dtype=np.int32,
)
flow_opposite = [0, 2, 1, 4, 3, 6, 5, 8, 7, 10, 9, 12, 11, 14, 13, 16, 15, 18, 17]
flow_weight = [1.0 / 3.0] + [1.0 / 18.0] * 6 + [1.0 / 36.0] * 12
thermal_stencil_coefficient = [0.25] + [0.125] * 6
flow_rate = 1.2
interface_exchange = 0.5

x_up = (1, 7, 9, 11, 13)
x_down = (2, 8, 10, 12, 14)
y_up = (3, 15, 17, 7, 10)
y_down = (4, 16, 18, 8, 9)

HIGHEST = lax.Precision.HIGHEST
limit = 32 * 1024 * 1024


def sine_constants(size):
    counting = np.arange(1, size + 1, dtype=np.float64)
    sine = math.sqrt(2.0 / (size + 1)) * np.sin(
        math.pi * counting[:, None] * counting[None, :] / (size + 1)
    )
    values = 2.0 - 2.0 * np.cos(math.pi * counting / (size + 1))
    plane = np.kron(sine, sine)
    total = values[:, None] + (values[:, None] + values[None, :]).reshape(1, -1)
    return (
        sine.astype(np.float32),
        plane.astype(np.float32),
        total.astype(np.float32),
        np.ascontiguousarray(np.broadcast_to(sine[:, :1], total.shape)).astype(np.float32),
    )


def dot(a, b, precision=None):
    return lax.dot_general(
        a, b, (((1,), (0,)), ((), ())), precision=precision, preferred_element_type=jnp.float32
    )


def dot_last(a, b):
    return lax.dot_general(a, b, (((1,), (1,)), ((), ())), preferred_element_type=jnp.float32)


def parts_of(value, count):
    parts = []
    for _ in range(count):
        part = value.astype(jnp.bfloat16)
        parts.append(part)
        value = value - part.astype(jnp.float32)
    return parts


def one_hot(row, size):
    numbers = lax.broadcasted_iota(jnp.int32, (size, row.shape[1]), 0)
    return jnp.where(numbers == row, 1.0, 0.0).astype(jnp.bfloat16)


def first_kernel(me_ref, out_ref):
    out_ref[...] = jnp.full(out_ref.shape, me_ref[0], jnp.int32)


def collide_kernel(
    flow_ref, heat_ref, mask_ref, rate_ref, _,
    post_ref, heat_post_ref, xu_ref, xd_ref, yu_ref, yd_ref,
):
    wide_x, wide_y = flow_ref.shape[1], flow_ref.shape[2]
    for x in range(wide_x):
        f = [flow_ref[i, x] for i in range(19)]
        density = functools.reduce(lambda a, b: a + b, f)
        momentum = []
        for axis in range(3):
            plus = [f[i] for i in range(19) if flow_velocity[i, axis] > 0]
            minus = [f[i] for i in range(19) if flow_velocity[i, axis] < 0]
            momentum.append(
                functools.reduce(lambda a, b: a + b, plus)
                - functools.reduce(lambda a, b: a + b, minus)
            )
        inverse = 1.0 / density
        speed = [m * inverse for m in momentum]
        square = speed[0] * speed[0] + speed[1] * speed[1] + speed[2] * speed[2]
        base = 1.0 - 1.5 * square
        is_fluid = mask_ref[x] == 1

        def along(i):
            total = None
            for axis in range(3):
                c = int(flow_velocity[i, axis])
                if c == 0:
                    continue
                term = speed[axis] if c > 0 else -speed[axis]
                total = term if total is None else total + term
            return total

        weighted = {w: density * w for w in set(flow_weight)}
        post = [None] * 19
        for i in [0] + list(range(1, 19, 2)):
            scale = weighted[flow_weight[i]]
            if i == 0:
                post[0] = jnp.where(is_fluid, f[0] - flow_rate * (f[0] - scale * base), f[0])
                continue
            cu = along(i)
            even = base + 4.5 * (cu * cu)
            odd = 3.0 * cu
            for k, balanced in ((i, scale * (even + odd)), (i + 1, scale * (even - odd))):
                post[k] = jnp.where(
                    is_fluid, f[k] - flow_rate * (f[k] - balanced), f[flow_opposite[k]]
                )
        h = [heat_ref[i, x] for i in range(7)]
        warmth = functools.reduce(lambda a, b: a + b, h)
        rate = rate_ref[x]
        heat = []
        for i in range(7):
            scale = thermal_stencil_coefficient[i] * warmth
            balanced = scale if i == 0 else scale * (1.0 + 4.0 * along(i))
            heat.append(jnp.where(is_fluid, h[i] - rate * (h[i] - balanced), h[flow_opposite[i]]))
        for i in range(19):
            post_ref[i, x] = post[i]
        for i in range(7):
            heat_post_ref[i, x] = heat[i]
        if x == wide_x - 1:
            for slot, part in enumerate([heat[1]] + [post[i] for i in x_up]):
                xu_ref[slot] = part
        if x == 0:
            for slot, part in enumerate([heat[2]] + [post[i] for i in x_down]):
                xd_ref[slot] = part
        last, row = slice(wide_y - 1, wide_y), slice(x, x + 1)
        for slot, part in enumerate([heat[3]] + [post[i] for i in y_up]):
            yu_ref[slot, row, :] = part[last]
        for slot, part in enumerate([heat[4]] + [post[i] for i in y_down]):
            yd_ref[slot, row, :] = part[0:1]


def block_kernel(
    source_ref, site_ref, owner_ref, node_ref, uptake_ref, wide_ref,
    sine_ref, plane_ref, total_ref, first_ref,
    cube_ref, reply_ref, part_ref, at_plane_ref, at_depth_ref, at_owner_ref, at_node_ref,
    *, n_wide, face, depth,
):
    sine, plane = sine_ref[...], plane_ref[...]
    inverse = 1.0 / (total_ref[...] + uptake_ref[0])
    spectral = dot(dot(sine, source_ref[0], HIGHEST), plane, HIGHEST) * inverse
    cube = dot(dot(sine, spectral, HIGHEST), plane, HIGHEST)
    reply = dot(sine, first_ref[...] * inverse, HIGHEST)
    cube_ref[...] = cube
    reply_ref[...] = reply
    owners, nodes, sites = owner_ref[...], node_ref[...], site_ref[...]
    number = ((owners * n_wide + wide_ref[0]) * face + nodes).astype(jnp.float32)
    half = face // 2
    part_ref[...] = jnp.concatenate(
        [
            number, cube[0:1, 0:half], cube[0:1, half:], reply[0:1, 0:half], reply[0:1, half:],
            number,
        ],
        axis=0,
    )
    flat = lambda rows: jnp.concatenate([rows[0:1], rows[1:2]], axis=1)
    at_plane_ref[...] = one_hot(flat(sites // depth), at_plane_ref.shape[0])
    at_depth_ref[...] = one_hot(flat(sites % depth), at_depth_ref.shape[0])
    at_owner_ref[...] = one_hot(flat(owners), at_owner_ref.shape[0])
    at_node_ref[...] = one_hot(flat(nodes), at_node_ref.shape[0])


def moved_x(rows, direction, edge):
    size = rows.shape[0]
    numbers = lax.broadcasted_iota(jnp.int32, rows.shape, 0)
    if direction > 0:
        return jnp.where(numbers == 0, edge, pltpu.roll(rows, 1, 0))
    return jnp.where(numbers == size - 1, edge, pltpu.roll(rows, size - 1, 0))


def rim_kernel(yu_raw_ref, yd_raw_ref, xu_ref, xd_ref, yu_ref, yd_ref):
    last = xu_ref.shape[1] - 1
    for raw_ref, out_ref, names, y in (
        (yu_raw_ref, yu_ref, y_up, last),
        (yd_raw_ref, yd_ref, y_down, 0),
    ):
        out_ref[0] = raw_ref[0]
        for slot, i in enumerate(names, 1):
            direction = int(flow_velocity[i, 0])
            rows = raw_ref[slot]
            if direction:
                edges, at = (xu_ref, x_up) if direction > 0 else (xd_ref, x_down)
                rows = moved_x(rows, direction, edges[1 + at.index(i), y : y + 1, :])
            out_ref[slot] = rows


def shifted_y(value, direction, edge):
    size = value.shape[0]
    rows = lax.broadcasted_iota(jnp.int32, value.shape, 0)
    if direction > 0:
        return jnp.where(rows == 0, edge, pltpu.roll(value, 1, 0))
    return jnp.where(rows == size - 1, edge, pltpu.roll(value, size - 1, 0))


def shifted_z(value, direction):
    if direction == 0:
        return value
    return pltpu.roll(value, 1 if direction > 0 else value.shape[1] - 1, 1)


def warmth_kernel(
    heat_post_ref, xu_ref, xd_ref, yu_ref, yd_ref, part_ref, at_plane_ref, at_depth_ref,
    passed_ref, warmth_ref, send_ref,
):
    wide_x, wide_y, depth = heat_post_ref.shape[1:]
    planes = []
    for x in range(wide_x):
        passed = [
            heat_post_ref[0, x],
            xu_ref[0] if x == 0 else heat_post_ref[1, x - 1],
            xd_ref[0] if x == wide_x - 1 else heat_post_ref[2, x + 1],
            shifted_y(heat_post_ref[3, x], 1, yu_ref[0, x : x + 1, :]),
            shifted_y(heat_post_ref[4, x], -1, yd_ref[0, x : x + 1, :]),
            shifted_z(heat_post_ref[5, x], 1),
            shifted_z(heat_post_ref[6, x], -1),
        ]
        for i in range(7):
            passed_ref[i, x] = passed[i]
        planes.append(functools.reduce(lambda a, b: a + b, passed))
    field = jnp.concatenate(planes, axis=0)
    count = wide_x * wide_y
    picked = dot(jnp.concatenate(parts_of(field, 3), axis=0), at_depth_ref[...])
    picked = picked[0:count] + picked[count : 2 * count] + picked[2 * count :]
    warmth = jnp.sum(picked * at_plane_ref[...].astype(jnp.float32), axis=0, keepdims=True)
    warmth_ref[...] = warmth
    half = warmth.shape[1] // 2
    message = jnp.concatenate([warmth[:, 0:half], warmth[:, half:], part_ref[0:6]], axis=0)
    for peer in range(send_ref.shape[0]):
        send_ref[peer] = message


def stream_kernel(post_ref, xu_ref, xd_ref, yu_ref, yd_ref, out_ref):
    wide_x = post_ref.shape[1]
    for i in range(19):
        cx, cy, cz = (int(c) for c in flow_velocity[i])
        for x in range(wide_x):
            if cx > 0 and x == 0:
                value = xu_ref[1 + x_up.index(i)]
            elif cx < 0 and x == wide_x - 1:
                value = xd_ref[1 + x_down.index(i)]
            else:
                value = post_ref[i, x - cx]
            if cy:
                edges, at = (yu_ref, y_up) if cy > 0 else (yd_ref, y_down)
                value = shifted_y(value, cy, edges[1 + at.index(i), x : x + 1, :])
            out_ref[i, x] = shifted_z(value, cz)


def finish_kernel(
    got_ref, passed_ref, warmth_ref, at_plane_ref, at_depth_ref, at_owner_ref, at_node_ref,
    me_ref, cube_ref, reply_ref, plane_ref,
    heat_ref, cube_out_ref,
    high_ref, low_ref, owner_rows_ref, node_columns_ref, table_ref, *, n_wide, face,
):
    peers, depth = got_ref.shape[0] // 8, got_ref.shape[1]
    wide_x, wide_y = passed_ref.shape[1:3]
    bits = lambda row: got_ref[pl.ds(row, peers, stride=8), :]
    for half in range(2):
        temperature = bits(half)
        high = temperature.astype(jnp.bfloat16).astype(jnp.float32)
        high_ref[half] = high
        low_ref[half] = temperature - high
        number = bits(2 + half).astype(jnp.int32)
        owner_rows_ref[half] = (number // (n_wide * face)).astype(jnp.float32)
        node_columns_ref[half] = (number % face).astype(jnp.float32).T

    def spread(ref, half, d):
        row = ref[half, d : d + 1, :]
        return jnp.broadcast_to(row, (16, depth)).astype(jnp.bfloat16)

    numbers = lax.broadcasted_iota(jnp.int32, (16, depth), 0).astype(jnp.float32)
    lanes = lax.broadcasted_iota(jnp.int32, (depth, face), 1).astype(jnp.float32)
    lanes = lanes.astype(jnp.bfloat16)
    zero, one = jnp.bfloat16(0), jnp.bfloat16(1)
    owner_groups = -(-peers // 16)
    wanted = [(numbers + 16.0 * g).astype(jnp.bfloat16) for g in range(owner_groups)]
    both = jnp.zeros((2 * 16 * owner_groups, face), jnp.float32)
    chunk = math.gcd(peers, 8)
    for start in range(0, peers, chunk):
        left, right = [], []
        for d in range(start, start + chunk):
            for half in range(2):
                owner = spread(owner_rows_ref, half, d)
                high, low = spread(high_ref, half, d), spread(low_ref, half, d)
                hits = [owner == w for w in wanted]
                left.append(
                    jnp.concatenate(
                        [jnp.where(hit, high, zero) for hit in hits]
                        + [jnp.where(hit, low, zero) for hit in hits],
                        axis=0,
                    )
                )
                node = node_columns_ref[half, :, d : d + 1].astype(jnp.bfloat16)
                hit = jnp.broadcast_to(node, (depth, face)) == lanes
                right.append(jnp.where(hit, one, zero))
        both = both + dot(jnp.concatenate(left, axis=1), jnp.concatenate(right, axis=0))
    table = interface_exchange * (both[0:peers] + both[16 * owner_groups :][0:peers])
    plane = plane_ref[...]
    spectral = dot(table, plane, HIGHEST)
    table_ref[...] = spectral
    reply = jnp.concatenate([bits(6), bits(7)], axis=1)
    own = table_ref[pl.ds(me_ref[0], 1), :]
    answers = dot(
        jnp.concatenate([spectral * reply, reply_ref[...] * own], axis=0), plane, HIGHEST
    )
    surface = answers[0:peers] + jnp.concatenate([bits(4), bits(5)], axis=1)
    cube_out_ref[0] = cube_ref[...] + answers[peers:]

    picked = dot(jnp.concatenate(parts_of(surface, 3), axis=0), at_node_ref[...])
    picked = picked[0:peers] + picked[peers : 2 * peers] + picked[2 * peers :]
    boundary = jnp.sum(picked * at_owner_ref[...].astype(jnp.float32), axis=0, keepdims=True)
    flux = interface_exchange * (boundary - warmth_ref[...])
    count = wide_x * wide_y
    at_plane = at_plane_ref[...]
    flux_parts = [
        at_plane * jnp.broadcast_to(part, at_plane.shape) for part in parts_of(flux, 3)
    ]
    gain = dot_last(jnp.concatenate(flux_parts, axis=0), at_depth_ref[...])
    gain = gain[0:count] + gain[count : 2 * count] + gain[2 * count :]
    for x in range(wide_x):
        rows = gain[x * wide_y : (x + 1) * wide_y]
        for i in range(7):
            heat_ref[i, x] = passed_ref[i, x] + thermal_stencil_coefficient[i] * rows


def call(kernel, shapes, *operands, smem=(), scratch=(), cost=1000000):
    spaces = [pltpu.SMEM if i in smem else pltpu.VMEM for i in range(len(operands))]
    moved = sum(4 * math.prod(o.shape) for o in list(operands) + list(shapes))
    return pl.pallas_call(
        kernel,
        out_shape=list(shapes),
        in_specs=[pl.BlockSpec(memory_space=space) for space in spaces],
        out_specs=[pl.BlockSpec(memory_space=pltpu.VMEM) for _ in shapes],
        scratch_shapes=list(scratch),
        compiler_params=pltpu.CompilerParams(vmem_limit_bytes=limit),
        cost_estimate=pl.CostEstimate(flops=cost, bytes_accessed=moved, transcendentals=0),
    )(*operands)


def f32(*shape):
    return jax.ShapeDtypeStruct(shape, jnp.float32)


def b16(*shape):
    return jax.ShapeDtypeStruct(shape, jnp.bfloat16)


def per_device(
    flow_state,
    thermal_distributions_current,
    fluid_mask,
    heat_rate,
    solid_source,
    cube_uptake_coefficients,
    owner_of,
    emitting_grid_site,
    target_node,
):
    bx, by, nz = fluid_mask.shape
    size, face = solid_source.shape[1:]
    peers, n_wide = lax.axis_size("narrow"), lax.axis_size("wide")
    rows = emitting_grid_site.shape[0]
    site = emitting_grid_site.reshape(2, rows // 2)
    owner = owner_of.reshape(2, rows // 2)
    node = target_node.reshape(2, rows // 2)
    me = lax.axis_index("narrow").astype(jnp.int32).reshape(1)
    wide = lax.axis_index("wide").astype(jnp.int32).reshape(1)
    sine, plane, total, first = (jnp.asarray(c) for c in sine_constants(size))

    (early,) = call(
        first_kernel, (jax.ShapeDtypeStruct((8, nz), jnp.int32),), me, smem=(0,), cost=10**10
    )
    post, heat_post, xu, xd, yu, yd = call(
        collide_kernel,
        (
            f32(19, bx, by, nz), f32(7, bx, by, nz), f32(6, by, nz), f32(6, by, nz),
            f32(6, bx, nz), f32(6, bx, nz),
        ),
        flow_state, thermal_distributions_current, fluid_mask, heat_rate, early,
    )
    cube, reply, part, at_plane, at_depth, at_owner, at_node = call(
        functools.partial(block_kernel, n_wide=n_wide, face=face, depth=nz),
        (
            f32(size, face), f32(size, face), f32(8, face // 2),
            b16(bx * by, rows), b16(nz, rows), b16(peers, rows), b16(face, rows),
        ),
        solid_source, site, owner, node, cube_uptake_coefficients, wide,
        sine, plane, total, first,
        smem=(4, 5),
    )

    def send(block, axis, step):
        count = lax.axis_size(axis)
        return lax.ppermute(block, axis, [(i, (i + step) % count) for i in range(count)])

    xu, xd = send(xu, "narrow", 1), send(xd, "narrow", -1)
    yu, yd = call(rim_kernel, (f32(6, bx, nz), f32(6, bx, nz)), yu, yd, xu, xd)
    yu, yd = send(yu, "wide", 1), send(yd, "wide", -1)
    passed, warmth, message = call(
        warmth_kernel,
        (f32(7, bx, by, nz), f32(1, rows), f32(peers, 8, face // 2)),
        heat_post, xu, xd, yu, yd, part, at_plane, at_depth,
    )
    got = lax.all_to_all(message, "narrow", split_axis=0, concat_axis=0, tiled=True)
    (stream,) = call(stream_kernel, (f32(19, bx, by, nz),), post, xu, xd, yu, yd)
    heat, cubes = call(
        functools.partial(finish_kernel, n_wide=n_wide, face=face),
        (f32(7, bx, by, nz), f32(1, size, face)),
        got.reshape(peers * 8, face // 2), passed, warmth, at_plane, at_depth, at_owner, at_node,
        me, cube, reply, plane,
        smem=(7,),
        scratch=[pltpu.VMEM((2, peers, face // 2), jnp.float32)] * 3
        + [pltpu.VMEM((2, face // 2, peers), jnp.float32), pltpu.VMEM((peers, face), jnp.float32)],
    )
    return stream, heat, cubes


def solution(mesh):
    return jax.shard_map(
        per_device,
        mesh=mesh,
        in_specs=(
            P(None, "narrow", "wide", None),
            P(None, "narrow", "wide", None),
            P("narrow", "wide", None),
            P("narrow", "wide", None),
            P(("narrow", "wide"), None, None),
            P(("narrow", "wide")),
            P(("narrow", "wide"), None),
            P(("narrow", "wide")),
            P(("narrow", "wide")),
        ),
        out_specs=(
            P(None, "narrow", "wide", None),
            P(None, "narrow", "wide", None),
            P(("narrow", "wide"), None, None),
        ),
        check_vma=False,
    )
```

```python
import functools
import math

import jax
import jax.numpy as jnp
import numpy as np
from jax import lax
from jax.experimental import pallas as pl
from jax.experimental.pallas import tpu as pltpu
from jax.sharding import PartitionSpec as P

flow_velocity = np.array(
    [
        [0, 0, 0],
        [1, 0, 0],
        [-1, 0, 0],
        [0, 1, 0],
        [0, -1, 0],
        [0, 0, 1],
        [0, 0, -1],
        [1, 1, 0],
        [-1, -1, 0],
        [1, -1, 0],
        [-1, 1, 0],
        [1, 0, 1],
        [-1, 0, -1],
        [1, 0, -1],
        [-1, 0, 1],
        [0, 1, 1],
        [0, -1, -1],
        [0, 1, -1],
        [0, -1, 1],
    ],
    dtype=np.int32,
)
flow_opposite = [0, 2, 1, 4, 3, 6, 5, 8, 7, 10, 9, 12, 11, 14, 13, 16, 15, 18, 17]
flow_weight = [1.0 / 3.0] + [1.0 / 18.0] * 6 + [1.0 / 36.0] * 12
thermal_stencil_coefficient = [0.25] + [0.125] * 6
flow_rate = 1.2
interface_exchange = 0.5

x_up = (1, 7, 9, 11, 13)
x_down = (2, 8, 10, 12, 14)
y_up = (3, 15, 17)
y_down = (4, 16, 18)
diagonal_up = (7, 10)
diagonal_down = (8, 9)

HIGHEST = lax.Precision.HIGHEST
limit = 32 * 1024 * 1024


def sine_constants(size):
    counting = np.arange(1, size + 1, dtype=np.float64)
    sine = math.sqrt(2.0 / (size + 1)) * np.sin(
        math.pi * counting[:, None] * counting[None, :] / (size + 1)
    )
    values = 2.0 - 2.0 * np.cos(math.pi * counting / (size + 1))
    plane = np.kron(sine, sine)
    total = values[:, None] + (values[:, None] + values[None, :]).reshape(1, -1)
    return (
        sine.astype(np.float32),
        plane.astype(np.float32),
        total.astype(np.float32),
        np.ascontiguousarray(np.broadcast_to(sine[:, :1], total.shape)).astype(np.float32),
    )


def dot(a, b, precision=None):
    return lax.dot_general(
        a, b, (((1,), (0,)), ((), ())), precision=precision, preferred_element_type=jnp.float32
    )


def dot_last(a, b):
    return lax.dot_general(a, b, (((1,), (1,)), ((), ())), preferred_element_type=jnp.float32)


def parts_of(value, count):
    parts = []
    for _ in range(count):
        part = value.astype(jnp.bfloat16)
        parts.append(part)
        value = value - part.astype(jnp.float32)
    return parts


def one_hot(row, size):
    numbers = lax.broadcasted_iota(jnp.int32, (size, row.shape[1]), 0)
    return jnp.where(numbers == row, 1.0, 0.0).astype(jnp.bfloat16)


def first_kernel(me_ref, out_ref):
    out_ref[...] = jnp.full(out_ref.shape, me_ref[0], jnp.int32)


def collide_kernel(
    flow_ref, heat_ref, mask_ref, rate_ref, *refs
):
    post_ref, heat_post_ref, xu_ref, xd_ref, yu_ref, yd_ref, du_ref, dd_ref = refs[-8:]
    wide_x, wide_y = flow_ref.shape[1], flow_ref.shape[2]
    for x in range(wide_x):
        f = [flow_ref[i, x] for i in range(19)]
        density = functools.reduce(lambda a, b: a + b, f)
        momentum = []
        for axis in range(3):
            plus = [f[i] for i in range(19) if flow_velocity[i, axis] > 0]
            minus = [f[i] for i in range(19) if flow_velocity[i, axis] < 0]
            momentum.append(
                functools.reduce(lambda a, b: a + b, plus)
                - functools.reduce(lambda a, b: a + b, minus)
            )
        inverse = 1.0 / density
        speed = [m * inverse for m in momentum]
        square = speed[0] * speed[0] + speed[1] * speed[1] + speed[2] * speed[2]
        base = 1.0 - 1.5 * square
        is_fluid = mask_ref[x] == 1

        def along(i):
            total = None
            for axis in range(3):
                c = int(flow_velocity[i, axis])
                if c == 0:
                    continue
                term = speed[axis] if c > 0 else -speed[axis]
                total = term if total is None else total + term
            return total

        weighted = {w: density * w for w in set(flow_weight)}
        post = [None] * 19
        for i in [0] + list(range(1, 19, 2)):
            scale = weighted[flow_weight[i]]
            if i == 0:
                post[0] = jnp.where(is_fluid, f[0] - flow_rate * (f[0] - scale * base), f[0])
                continue
            cu = along(i)
            even = base + 4.5 * (cu * cu)
            odd = 3.0 * cu
            for k, balanced in ((i, scale * (even + odd)), (i + 1, scale * (even - odd))):
                post[k] = jnp.where(
                    is_fluid, f[k] - flow_rate * (f[k] - balanced), f[flow_opposite[k]]
                )
        h = [heat_ref[i, x] for i in range(7)]
        warmth = functools.reduce(lambda a, b: a + b, h)
        rate = rate_ref[x]
        heat = []
        for i in range(7):
            scale = thermal_stencil_coefficient[i] * warmth
            balanced = scale if i == 0 else scale * (1.0 + 4.0 * along(i))
            heat.append(jnp.where(is_fluid, h[i] - rate * (h[i] - balanced), h[flow_opposite[i]]))
        for i in range(19):
            post_ref[i, x] = post[i]
        for i in range(7):
            heat_post_ref[i, x] = heat[i]
        if x == wide_x - 1:
            for slot, part in enumerate([heat[1]] + [post[i] for i in x_up]):
                xu_ref[slot] = part
        if x == 0:
            for slot, part in enumerate([heat[2]] + [post[i] for i in x_down]):
                xd_ref[slot] = part
        last, row = slice(wide_y - 1, wide_y), slice(x, x + 1)
        for slot, part in enumerate([heat[3]] + [post[i] for i in y_up]):
            yu_ref[slot, row, :] = part[last]
        for slot, part in enumerate([heat[4]] + [post[i] for i in y_down]):
            yd_ref[slot, row, :] = part[0:1]
        for slot, i in enumerate(diagonal_up):
            du_ref[slot, row, :] = post[i][last]
        for slot, i in enumerate(diagonal_down):
            dd_ref[slot, row, :] = post[i][0:1]


def block_kernel(
    source_ref, site_ref, owner_ref, node_ref, uptake_ref, wide_ref,
    sine_ref, plane_ref, total_ref, first_ref,
    cube_ref, reply_ref, part_ref, at_plane_ref, at_depth_ref, at_owner_ref, at_node_ref,
    *, n_wide, face, depth,
):
    sine, plane = sine_ref[...], plane_ref[...]
    inverse = 1.0 / (total_ref[...] + uptake_ref[...])
    spectral = dot(dot(sine, source_ref[0], HIGHEST), plane, HIGHEST) * inverse
    cube = dot(dot(sine, spectral, HIGHEST), plane, HIGHEST)
    reply = dot(sine, first_ref[...] * inverse, HIGHEST)
    cube_ref[...] = cube
    reply_ref[...] = reply
    owners, nodes, sites = owner_ref[...], node_ref[...], site_ref[...]
    number = ((owners * n_wide + wide_ref[0]) * face + nodes).astype(jnp.float32)
    half = face // 2
    part_ref[...] = jnp.concatenate(
        [
            number, cube[0:1, 0:half], cube[0:1, half:], reply[0:1, 0:half], reply[0:1, half:],
            number,
        ],
        axis=0,
    )
    flat = lambda rows: jnp.concatenate([rows[0:1], rows[1:2]], axis=1)
    at_plane_ref[...] = one_hot(flat(sites // depth), at_plane_ref.shape[0])
    at_depth_ref[...] = one_hot(flat(sites % depth), at_depth_ref.shape[0])
    at_owner_ref[...] = one_hot(flat(owners), at_owner_ref.shape[0])
    at_node_ref[...] = one_hot(flat(nodes), at_node_ref.shape[0])


def moved_x(rows, direction, edge):
    size = rows.shape[0]
    numbers = lax.broadcasted_iota(jnp.int32, rows.shape, 0)
    if direction > 0:
        return jnp.where(numbers == 0, edge, pltpu.roll(rows, 1, 0))
    return jnp.where(numbers == size - 1, edge, pltpu.roll(rows, size - 1, 0))


def rim_kernel(du_raw_ref, dd_raw_ref, xu_ref, xd_ref, du_ref, dd_ref):
    last = xu_ref.shape[1] - 1
    for raw_ref, out_ref, names, y in (
        (du_raw_ref, du_ref, diagonal_up, last),
        (dd_raw_ref, dd_ref, diagonal_down, 0),
    ):
        for slot, i in enumerate(names):
            direction = int(flow_velocity[i, 0])
            edges, at = (xu_ref, x_up) if direction > 0 else (xd_ref, x_down)
            edge = edges[1 + at.index(i), y : y + 1, :]
            out_ref[slot] = moved_x(raw_ref[slot], direction, edge)


def shifted_y(value, direction, edge):
    size = value.shape[0]
    rows = lax.broadcasted_iota(jnp.int32, value.shape, 0)
    if direction > 0:
        return jnp.where(rows == 0, edge, pltpu.roll(value, 1, 0))
    return jnp.where(rows == size - 1, edge, pltpu.roll(value, size - 1, 0))


def shifted_z(value, direction):
    if direction == 0:
        return value
    return pltpu.roll(value, 1 if direction > 0 else value.shape[1] - 1, 1)


def warmth_kernel(
    heat_post_ref, xu_ref, xd_ref, yu_ref, yd_ref, part_ref, at_plane_ref, at_depth_ref,
    passed_ref, warmth_ref, send_ref,
):
    wide_x, wide_y, depth = heat_post_ref.shape[1:]
    planes = []
    for x in range(wide_x):
        passed = [
            heat_post_ref[0, x],
            xu_ref[0] if x == 0 else heat_post_ref[1, x - 1],
            xd_ref[0] if x == wide_x - 1 else heat_post_ref[2, x + 1],
            shifted_y(heat_post_ref[3, x], 1, yu_ref[0, x : x + 1, :]),
            shifted_y(heat_post_ref[4, x], -1, yd_ref[0, x : x + 1, :]),
            shifted_z(heat_post_ref[5, x], 1),
            shifted_z(heat_post_ref[6, x], -1),
        ]
        for i in range(7):
            passed_ref[i, x] = passed[i]
        planes.append(functools.reduce(lambda a, b: a + b, passed))
    field = jnp.concatenate(planes, axis=0)
    count = wide_x * wide_y
    picked = dot(jnp.concatenate(parts_of(field, 3), axis=0), at_depth_ref[...])
    picked = picked[0:count] + picked[count : 2 * count] + picked[2 * count :]
    warmth = jnp.sum(picked * at_plane_ref[...].astype(jnp.float32), axis=0, keepdims=True)
    warmth_ref[...] = warmth
    half = warmth.shape[1] // 2
    message = jnp.concatenate([warmth[:, 0:half], warmth[:, half:], part_ref[0:6]], axis=0)
    for peer in range(send_ref.shape[0]):
        send_ref[peer] = message


def stream_kernel(post_ref, xu_ref, xd_ref, yu_ref, yd_ref, du_ref, dd_ref, out_ref):
    wide_x = post_ref.shape[1]
    for i in range(19):
        cx, cy, cz = (int(c) for c in flow_velocity[i])
        for x in range(wide_x):
            if cx > 0 and x == 0:
                value = xu_ref[1 + x_up.index(i)]
            elif cx < 0 and x == wide_x - 1:
                value = xd_ref[1 + x_down.index(i)]
            else:
                value = post_ref[i, x - cx]
            if cy:
                if cx:
                    edges = du_ref if cy > 0 else dd_ref
                    slot = (diagonal_up if cy > 0 else diagonal_down).index(i)
                else:
                    edges = yu_ref if cy > 0 else yd_ref
                    slot = 1 + (y_up if cy > 0 else y_down).index(i)
                value = shifted_y(value, cy, edges[slot, x : x + 1, :])
            out_ref[i, x] = shifted_z(value, cz)


def finish_kernel(
    got_ref, passed_ref, warmth_ref, at_plane_ref, at_depth_ref, at_owner_ref, at_node_ref,
    me_ref, cube_ref, reply_ref, plane_ref,
    heat_ref, cube_out_ref,
    high_ref, low_ref, owner_rows_ref, node_columns_ref, table_ref, *, n_wide, face,
):
    peers, depth = got_ref.shape[0] // 8, got_ref.shape[1]
    wide_x, wide_y = passed_ref.shape[1:3]
    bits = lambda row: got_ref[pl.ds(row, peers, stride=8), :]
    for half in range(2):
        temperature = bits(half)
        high = temperature.astype(jnp.bfloat16).astype(jnp.float32)
        high_ref[half] = high
        low_ref[half] = temperature - high
        number = bits(2 + half).astype(jnp.int32)
        owner_rows_ref[half] = (number // (n_wide * face)).astype(jnp.float32)
        node_columns_ref[half] = (number % face).astype(jnp.float32).T

    def spread(ref, half, d):
        row = ref[half, d : d + 1, :]
        return jnp.broadcast_to(row, (16, depth)).astype(jnp.bfloat16)

    numbers = lax.broadcasted_iota(jnp.int32, (16, depth), 0).astype(jnp.float32)
    lanes = lax.broadcasted_iota(jnp.int32, (depth, face), 1).astype(jnp.float32)
    lanes = lanes.astype(jnp.bfloat16)
    zero, one = jnp.bfloat16(0), jnp.bfloat16(1)
    owner_groups = -(-peers // 16)
    wanted = [(numbers + 16.0 * g).astype(jnp.bfloat16) for g in range(owner_groups)]
    both = jnp.zeros((2 * 16 * owner_groups, face), jnp.float32)
    chunk = math.gcd(peers, 8)
    for start in range(0, peers, chunk):
        left, right = [], []
        for d in range(start, start + chunk):
            for half in range(2):
                owner = spread(owner_rows_ref, half, d)
                high, low = spread(high_ref, half, d), spread(low_ref, half, d)
                hits = [owner == w for w in wanted]
                left.append(
                    jnp.concatenate(
                        [jnp.where(hit, high, zero) for hit in hits]
                        + [jnp.where(hit, low, zero) for hit in hits],
                        axis=0,
                    )
                )
                node = node_columns_ref[half, :, d : d + 1].astype(jnp.bfloat16)
                hit = jnp.broadcast_to(node, (depth, face)) == lanes
                right.append(jnp.where(hit, one, zero))
        both = both + dot(jnp.concatenate(left, axis=1), jnp.concatenate(right, axis=0))
    table = interface_exchange * (both[0:peers] + both[16 * owner_groups :][0:peers])
    plane = plane_ref[...]
    spectral = dot(table, plane, HIGHEST)
    table_ref[...] = spectral
    reply = jnp.concatenate([bits(6), bits(7)], axis=1)
    own = table_ref[pl.ds(me_ref[0], 1), :]
    answers = dot(
        jnp.concatenate([spectral * reply, reply_ref[...] * own], axis=0), plane, HIGHEST
    )
    surface = answers[0:peers] + jnp.concatenate([bits(4), bits(5)], axis=1)
    cube_out_ref[0] = cube_ref[...] + answers[peers:]

    picked = dot(jnp.concatenate(parts_of(surface, 3), axis=0), at_node_ref[...])
    picked = picked[0:peers] + picked[peers : 2 * peers] + picked[2 * peers :]
    boundary = jnp.sum(picked * at_owner_ref[...].astype(jnp.float32), axis=0, keepdims=True)
    flux = interface_exchange * (boundary - warmth_ref[...])
    count = wide_x * wide_y
    at_plane = at_plane_ref[...]
    flux_parts = [
        at_plane * jnp.broadcast_to(part, at_plane.shape) for part in parts_of(flux, 3)
    ]
    gain = dot_last(jnp.concatenate(flux_parts, axis=0), at_depth_ref[...])
    gain = gain[0:count] + gain[count : 2 * count] + gain[2 * count :]
    for x in range(wide_x):
        rows = gain[x * wide_y : (x + 1) * wide_y]
        for i in range(7):
            heat_ref[i, x] = passed_ref[i, x] + thermal_stencil_coefficient[i] * rows


def call(kernel, shapes, *operands, smem=(), scratch=(), cost=1000000):
    spaces = [pltpu.SMEM if i in smem else pltpu.VMEM for i in range(len(operands))]
    moved = sum(4 * math.prod(o.shape) for o in list(operands) + list(shapes))
    return pl.pallas_call(
        kernel,
        out_shape=list(shapes),
        in_specs=[pl.BlockSpec(memory_space=space) for space in spaces],
        out_specs=[pl.BlockSpec(memory_space=pltpu.VMEM) for _ in shapes],
        scratch_shapes=list(scratch),
        compiler_params=pltpu.CompilerParams(vmem_limit_bytes=limit),
        cost_estimate=pl.CostEstimate(flops=cost, bytes_accessed=moved, transcendentals=0),
    )(*operands)


def f32(*shape):
    return jax.ShapeDtypeStruct(shape, jnp.float32)


def b16(*shape):
    return jax.ShapeDtypeStruct(shape, jnp.bfloat16)


def per_device(
    flow_state,
    thermal_distributions_current,
    fluid_mask,
    heat_rate,
    solid_source,
    cube_uptake_coefficients,
    owner_of,
    emitting_grid_site,
    target_node,
):
    bx, by, nz = fluid_mask.shape
    size, face = solid_source.shape[1:]
    peers, n_wide = lax.axis_size("narrow"), lax.axis_size("wide")
    rows = emitting_grid_site.shape[0]
    site = emitting_grid_site.reshape(2, rows // 2)
    owner = owner_of.reshape(2, rows // 2)
    node = target_node.reshape(2, rows // 2)
    me = lax.axis_index("narrow").astype(jnp.int32).reshape(1)
    wide = lax.axis_index("wide").astype(jnp.int32).reshape(1)
    sine, plane, total, first = (jnp.asarray(c) for c in sine_constants(size))

    (early,) = call(
        first_kernel, (jax.ShapeDtypeStruct((8, nz), jnp.int32),), me, smem=(0,), cost=10**10
    )
    uptake = cube_uptake_coefficients.reshape(1, 1)
    post, heat_post, xu, xd, yu, yd, du, dd = call(
        collide_kernel,
        (
            f32(19, bx, by, nz), f32(7, bx, by, nz), f32(6, by, nz), f32(6, by, nz),
            f32(4, bx, nz), f32(4, bx, nz), f32(2, bx, nz), f32(2, bx, nz),
        ),
        flow_state, thermal_distributions_current, fluid_mask, heat_rate, early,
        solid_source, site, owner, node,
    )
    cube, reply, part, at_plane, at_depth, at_owner, at_node = call(
        functools.partial(block_kernel, n_wide=n_wide, face=face, depth=nz),
        (
            f32(size, face), f32(size, face), f32(8, face // 2),
            b16(bx * by, rows), b16(nz, rows), b16(peers, rows), b16(face, rows),
        ),
        solid_source, site, owner, node, uptake, wide, sine, plane, total, first,
        smem=(5,),
        cost=10**10,
    )

    def send(block, axis, step):
        count = lax.axis_size(axis)
        return lax.ppermute(block, axis, [(i, (i + step) % count) for i in range(count)])

    xu, xd = send(xu, "narrow", 1), send(xd, "narrow", -1)
    yu, yd = send(yu, "wide", 1), send(yd, "wide", -1)
    passed, warmth, message = call(
        warmth_kernel,
        (f32(7, bx, by, nz), f32(1, rows), f32(peers, 8, face // 2)),
        heat_post, xu, xd, yu, yd, part, at_plane, at_depth,
    )
    got = lax.all_to_all(message, "narrow", split_axis=0, concat_axis=0, tiled=True)
    du, dd = call(rim_kernel, (f32(2, bx, nz), f32(2, bx, nz)), du, dd, xu, xd)
    du, dd = send(du, "wide", 1), send(dd, "wide", -1)
    (stream,) = call(
        stream_kernel, (f32(19, bx, by, nz),), post, xu, xd, yu, yd, du, dd
    )
    heat, cubes = call(
        functools.partial(finish_kernel, n_wide=n_wide, face=face),
        (f32(7, bx, by, nz), f32(1, size, face)),
        got.reshape(peers * 8, face // 2), passed, warmth, at_plane, at_depth, at_owner, at_node,
        me, cube, reply, plane,
        smem=(7,),
        scratch=[pltpu.VMEM((2, peers, face // 2), jnp.float32)] * 3
        + [pltpu.VMEM((2, face // 2, peers), jnp.float32), pltpu.VMEM((peers, face), jnp.float32)],
    )
    return stream, heat, cubes


def solution(mesh):
    return jax.shard_map(
        per_device,
        mesh=mesh,
        in_specs=(
            P(None, "narrow", "wide", None),
            P(None, "narrow", "wide", None),
            P("narrow", "wide", None),
            P("narrow", "wide", None),
            P(("narrow", "wide"), None, None),
            P(("narrow", "wide")),
            P(("narrow", "wide"), None),
            P(("narrow", "wide")),
            P(("narrow", "wide")),
        ),
        out_specs=(
            P(None, "narrow", "wide", None),
            P(None, "narrow", "wide", None),
            P(("narrow", "wide"), None, None),
        ),
        check_vma=False,
    )
```

```python
import functools
import math

import jax
import jax.numpy as jnp
import numpy as np
from jax import lax
from jax.experimental import pallas as pl
from jax.experimental.pallas import tpu as pltpu
from jax.sharding import PartitionSpec as P

flow_velocity = np.array(
    [
        [0, 0, 0],
        [1, 0, 0],
        [-1, 0, 0],
        [0, 1, 0],
        [0, -1, 0],
        [0, 0, 1],
        [0, 0, -1],
        [1, 1, 0],
        [-1, -1, 0],
        [1, -1, 0],
        [-1, 1, 0],
        [1, 0, 1],
        [-1, 0, -1],
        [1, 0, -1],
        [-1, 0, 1],
        [0, 1, 1],
        [0, -1, -1],
        [0, 1, -1],
        [0, -1, 1],
    ],
    dtype=np.int32,
)
flow_opposite = [0, 2, 1, 4, 3, 6, 5, 8, 7, 10, 9, 12, 11, 14, 13, 16, 15, 18, 17]
flow_weight = [1.0 / 3.0] + [1.0 / 18.0] * 6 + [1.0 / 36.0] * 12
thermal_stencil_coefficient = [0.25] + [0.125] * 6
flow_rate = 1.2
interface_exchange = 0.5

x_up = (1, 7, 9, 11, 13)
x_down = (2, 8, 10, 12, 14)
y_up = (3, 15, 17)
y_down = (4, 16, 18)
diagonal_up = (7, 10)
diagonal_down = (8, 9)

HIGHEST = lax.Precision.HIGHEST
limit = 32 * 1024 * 1024


def sine_constants(size):
    counting = np.arange(1, size + 1, dtype=np.float64)
    sine = math.sqrt(2.0 / (size + 1)) * np.sin(
        math.pi * counting[:, None] * counting[None, :] / (size + 1)
    )
    values = 2.0 - 2.0 * np.cos(math.pi * counting / (size + 1))
    plane = np.kron(sine, sine)
    high = plane.astype(jnp.bfloat16)
    low = (plane - high.astype(np.float64)).astype(jnp.bfloat16)
    plane_parts = np.concatenate([high, high, low], axis=0)
    total = values[:, None] + (values[:, None] + values[None, :]).reshape(1, -1)
    return (
        sine.astype(np.float32),
        plane_parts,
        total.astype(np.float32),
        np.ascontiguousarray(np.broadcast_to(sine[:, :1], total.shape)).astype(np.float32),
    )


def dot(a, b, precision=None):
    return lax.dot_general(
        a, b, (((1,), (0,)), ((), ())), precision=precision, preferred_element_type=jnp.float32
    )


def dot_last(a, b):
    return lax.dot_general(a, b, (((1,), (1,)), ((), ())), preferred_element_type=jnp.float32)


def parts_of(value, count):
    parts = []
    for _ in range(count):
        part = value.astype(jnp.bfloat16)
        parts.append(part)
        value = value - part.astype(jnp.float32)
    return parts


def one_hot(row, size):
    numbers = lax.broadcasted_iota(jnp.int32, (size, row.shape[1]), 0)
    return jnp.where(numbers == row, 1.0, 0.0).astype(jnp.bfloat16)


def first_kernel(me_ref, out_ref):
    out_ref[...] = jnp.full(out_ref.shape, me_ref[0], jnp.int32)


def is_odd(me_ref, shape):
    return jnp.full(shape, me_ref[0] % 2, jnp.int32) == 1


def faces_along_x(me_ref, xa_ref, xb_ref):
    def pick(even_ref, odd_ref):
        def read(slot, rows=slice(None)):
            a, b = even_ref[slot, rows, :], odd_ref[slot, rows, :]
            return jnp.where(is_odd(me_ref, a.shape), b, a)

        return read

    return pick(xa_ref, xb_ref), pick(xb_ref, xa_ref)


def collide_kernel(me_ref, flow_ref, heat_ref, mask_ref, rate_ref, *refs):
    post_ref, heat_post_ref, xa_ref, xb_ref, yu_ref, yd_ref, du_ref, dd_ref = refs[-8:]
    wide_x, wide_y = flow_ref.shape[1], flow_ref.shape[2]
    for x in range(wide_x):
        f = [flow_ref[i, x] for i in range(19)]
        density = functools.reduce(lambda a, b: a + b, f)
        momentum = []
        for axis in range(3):
            plus = [f[i] for i in range(19) if flow_velocity[i, axis] > 0]
            minus = [f[i] for i in range(19) if flow_velocity[i, axis] < 0]
            momentum.append(
                functools.reduce(lambda a, b: a + b, plus)
                - functools.reduce(lambda a, b: a + b, minus)
            )
        inverse = 1.0 / density
        speed = [m * inverse for m in momentum]
        square = speed[0] * speed[0] + speed[1] * speed[1] + speed[2] * speed[2]
        base = 1.0 - 1.5 * square
        is_fluid = mask_ref[x] == 1

        def along(i):
            total = None
            for axis in range(3):
                c = int(flow_velocity[i, axis])
                if c == 0:
                    continue
                term = speed[axis] if c > 0 else -speed[axis]
                total = term if total is None else total + term
            return total

        weighted = {w: density * w for w in set(flow_weight)}
        post = [None] * 19
        for i in [0] + list(range(1, 19, 2)):
            scale = weighted[flow_weight[i]]
            if i == 0:
                post[0] = jnp.where(is_fluid, f[0] - flow_rate * (f[0] - scale * base), f[0])
                continue
            cu = along(i)
            even = base + 4.5 * (cu * cu)
            odd = 3.0 * cu
            for k, balanced in ((i, scale * (even + odd)), (i + 1, scale * (even - odd))):
                post[k] = jnp.where(
                    is_fluid, f[k] - flow_rate * (f[k] - balanced), f[flow_opposite[k]]
                )
        h = [heat_ref[i, x] for i in range(7)]
        warmth = functools.reduce(lambda a, b: a + b, h)
        rate = rate_ref[x]
        heat = []
        for i in range(7):
            scale = thermal_stencil_coefficient[i] * warmth
            balanced = scale if i == 0 else scale * (1.0 + 4.0 * along(i))
            heat.append(jnp.where(is_fluid, h[i] - rate * (h[i] - balanced), h[flow_opposite[i]]))
        for i in range(19):
            post_ref[i, x] = post[i]
        for i in range(7):
            heat_post_ref[i, x] = heat[i]
        if x == 0:
            down = [heat[2]] + [post[i] for i in x_down]
        if x == wide_x - 1:
            odd = is_odd(me_ref, heat[1].shape)
            for slot, (low, high) in enumerate(zip(down, [heat[1]] + [post[i] for i in x_up])):
                xa_ref[slot] = jnp.where(odd, high, low)
                xb_ref[slot] = jnp.where(odd, low, high)
        last, row = slice(wide_y - 1, wide_y), slice(x, x + 1)
        for slot, part in enumerate([heat[3]] + [post[i] for i in y_up]):
            yu_ref[slot, row, :] = part[last]
        for slot, part in enumerate([heat[4]] + [post[i] for i in y_down]):
            yd_ref[slot, row, :] = part[0:1]
        for slot, i in enumerate(diagonal_up):
            du_ref[slot, row, :] = post[i][last]
        for slot, i in enumerate(diagonal_down):
            dd_ref[slot, row, :] = post[i][0:1]


def by_plane(value, parts_ref):
    high, low = parts_of(value, 2)
    return dot(jnp.concatenate([high, low, high], axis=1), parts_ref[...])


def flat(rows):
    return jnp.concatenate([rows[0:1], rows[1:2]], axis=1)


def face_kernel(
    source_ref, site_ref, owner_ref, node_ref, uptake_ref, wide_ref,
    sine_ref, parts_ref, total_ref, first_ref, part_ref, at_plane_ref, at_depth_ref,
    *, n_wide, face, depth,
):
    first = first_ref[...]
    inverse = 1.0 / (total_ref[...] + uptake_ref[...])
    spectral = by_plane(dot(sine_ref[...], source_ref[0], HIGHEST), parts_ref) * inverse
    reply = jnp.sum(first * first * inverse, axis=0, keepdims=True)
    answer = jnp.sum(first * spectral, axis=0, keepdims=True)
    answer = by_plane(jnp.broadcast_to(answer, (8, face)), parts_ref)[0:1]
    sites = site_ref[...]
    number = (owner_ref[...] * n_wide + wide_ref[0]) * face + node_ref[...]
    number = number.astype(jnp.float32)
    half = face // 2
    part_ref[...] = jnp.concatenate(
        [
            number, answer[:, 0:half], answer[:, half:], reply[:, 0:half], reply[:, half:],
            number,
        ],
        axis=0,
    )
    at_plane_ref[...] = one_hot(flat(sites // depth), at_plane_ref.shape[0])
    at_depth_ref[...] = one_hot(flat(sites % depth), at_depth_ref.shape[0])


def block_kernel(
    source_ref, owner_ref, node_ref, uptake_ref, sine_ref, parts_ref, total_ref, first_ref, _,
    cube_ref, reply_ref, at_owner_ref, at_node_ref,
):
    sine = sine_ref[...]
    inverse = 1.0 / (total_ref[...] + uptake_ref[...])
    spectral = by_plane(dot(sine, source_ref[0], HIGHEST), parts_ref) * inverse
    cube_ref[...] = by_plane(dot(sine, spectral, HIGHEST), parts_ref)
    reply_ref[...] = dot(sine, first_ref[...] * inverse, HIGHEST)
    at_owner_ref[...] = one_hot(flat(owner_ref[...]), at_owner_ref.shape[0])
    at_node_ref[...] = one_hot(flat(node_ref[...]), at_node_ref.shape[0])


def moved_x(rows, direction, edge):
    size = rows.shape[0]
    numbers = lax.broadcasted_iota(jnp.int32, rows.shape, 0)
    if direction > 0:
        return jnp.where(numbers == 0, edge, pltpu.roll(rows, 1, 0))
    return jnp.where(numbers == size - 1, edge, pltpu.roll(rows, size - 1, 0))


def rim_kernel(me_ref, du_raw_ref, dd_raw_ref, xa_ref, xb_ref, du_ref, dd_ref):
    last = xa_ref.shape[1] - 1
    below, above = faces_along_x(me_ref, xa_ref, xb_ref)
    for raw_ref, out_ref, names, y in (
        (du_raw_ref, du_ref, diagonal_up, last),
        (dd_raw_ref, dd_ref, diagonal_down, 0),
    ):
        for slot, i in enumerate(names):
            direction = int(flow_velocity[i, 0])
            face, at = (below, x_up) if direction > 0 else (above, x_down)
            edge = face(1 + at.index(i), slice(y, y + 1))
            out_ref[slot] = moved_x(raw_ref[slot], direction, edge)


def shifted_y(value, direction, edge):
    size = value.shape[0]
    rows = lax.broadcasted_iota(jnp.int32, value.shape, 0)
    if direction > 0:
        return jnp.where(rows == 0, edge, pltpu.roll(value, 1, 0))
    return jnp.where(rows == size - 1, edge, pltpu.roll(value, size - 1, 0))


def shifted_z(value, direction):
    if direction == 0:
        return value
    return pltpu.roll(value, 1 if direction > 0 else value.shape[1] - 1, 1)


def warmth_kernel(
    me_ref, heat_post_ref, xa_ref, yd_ref, yu_ref, xb_ref, part_ref, at_plane_ref, at_depth_ref,
    passed_ref, warmth_ref, send_ref,
):
    wide_x, wide_y, depth = heat_post_ref.shape[1:]
    below, above = faces_along_x(me_ref, xa_ref, xb_ref)
    planes = []
    for x in range(wide_x):
        passed = [
            heat_post_ref[0, x],
            below(0) if x == 0 else heat_post_ref[1, x - 1],
            above(0) if x == wide_x - 1 else heat_post_ref[2, x + 1],
            shifted_y(heat_post_ref[3, x], 1, yu_ref[0, x : x + 1, :]),
            shifted_y(heat_post_ref[4, x], -1, yd_ref[0, x : x + 1, :]),
            shifted_z(heat_post_ref[5, x], 1),
            shifted_z(heat_post_ref[6, x], -1),
        ]
        for i in range(7):
            passed_ref[i, x] = passed[i]
        planes.append(functools.reduce(lambda a, b: a + b, passed))
    field = jnp.concatenate(planes, axis=0)
    count = wide_x * wide_y
    picked = dot(jnp.concatenate(parts_of(field, 3), axis=0), at_depth_ref[...])
    picked = picked[0:count] + picked[count : 2 * count] + picked[2 * count :]
    warmth = jnp.sum(picked * at_plane_ref[...].astype(jnp.float32), axis=0, keepdims=True)
    warmth_ref[...] = warmth
    half = warmth.shape[1] // 2
    message = jnp.concatenate([warmth[:, 0:half], warmth[:, half:], part_ref[0:6]], axis=0)
    for peer in range(send_ref.shape[0]):
        send_ref[peer] = message


def stream_kernel(
    me_ref, post_ref, xa_ref, yd_ref, yu_ref, xb_ref, dd_ref, du_ref, out_ref
):
    below, above = faces_along_x(me_ref, xa_ref, xb_ref)
    wide_x = post_ref.shape[1]
    for i in range(19):
        cx, cy, cz = (int(c) for c in flow_velocity[i])
        for x in range(wide_x):
            if cx > 0 and x == 0:
                value = below(1 + x_up.index(i))
            elif cx < 0 and x == wide_x - 1:
                value = above(1 + x_down.index(i))
            else:
                value = post_ref[i, x - cx]
            if cy:
                if cx:
                    edges = du_ref if cy > 0 else dd_ref
                    slot = (diagonal_up if cy > 0 else diagonal_down).index(i)
                else:
                    edges = yu_ref if cy > 0 else yd_ref
                    slot = 1 + (y_up if cy > 0 else y_down).index(i)
                value = shifted_y(value, cy, edges[slot, x : x + 1, :])
            out_ref[i, x] = shifted_z(value, cz)


def finish_kernel(
    got_ref, passed_ref, warmth_ref, at_plane_ref, at_depth_ref, at_owner_ref, at_node_ref,
    me_ref, cube_ref, reply_ref, parts_ref,
    heat_ref, cube_out_ref,
    high_ref, low_ref, owner_rows_ref, node_columns_ref, table_ref, *, n_wide, face,
):
    peers, depth = got_ref.shape[0] // 8, got_ref.shape[1]
    wide_x, wide_y = passed_ref.shape[1:3]
    bits = lambda row: got_ref[pl.ds(row, peers, stride=8), :]
    for half in range(2):
        temperature = bits(half)
        high = temperature.astype(jnp.bfloat16).astype(jnp.float32)
        high_ref[half] = high
        low_ref[half] = temperature - high
        number = bits(2 + half).astype(jnp.int32)
        owner_rows_ref[half] = (number // (n_wide * face)).astype(jnp.float32)
        node_columns_ref[half] = (number % face).astype(jnp.float32).T

    def spread(ref, half, d):
        row = ref[half, d : d + 1, :]
        return jnp.broadcast_to(row, (16, depth)).astype(jnp.bfloat16)

    numbers = lax.broadcasted_iota(jnp.int32, (16, depth), 0).astype(jnp.float32)
    lanes = lax.broadcasted_iota(jnp.int32, (depth, face), 1).astype(jnp.float32)
    lanes = lanes.astype(jnp.bfloat16)
    zero, one = jnp.bfloat16(0), jnp.bfloat16(1)
    owner_groups = -(-peers // 16)
    wanted = [(numbers + 16.0 * g).astype(jnp.bfloat16) for g in range(owner_groups)]
    both = jnp.zeros((2 * 16 * owner_groups, face), jnp.float32)
    chunk = math.gcd(peers, 8)
    for start in range(0, peers, chunk):
        left, right = [], []
        for d in range(start, start + chunk):
            for half in range(2):
                owner = spread(owner_rows_ref, half, d)
                high, low = spread(high_ref, half, d), spread(low_ref, half, d)
                hits = [owner == w for w in wanted]
                left.append(
                    jnp.concatenate(
                        [jnp.where(hit, high, zero) for hit in hits]
                        + [jnp.where(hit, low, zero) for hit in hits],
                        axis=0,
                    )
                )
                node = node_columns_ref[half, :, d : d + 1].astype(jnp.bfloat16)
                hit = jnp.broadcast_to(node, (depth, face)) == lanes
                right.append(jnp.where(hit, one, zero))
        both = both + dot(jnp.concatenate(left, axis=1), jnp.concatenate(right, axis=0))
    table = interface_exchange * (both[0:peers] + both[16 * owner_groups :][0:peers])
    spectral = by_plane(table, parts_ref)
    table_ref[...] = spectral
    reply = jnp.concatenate([bits(6), bits(7)], axis=1)
    own = table_ref[pl.ds(me_ref[0], 1), :]
    answers = by_plane(
        jnp.concatenate([spectral * reply, reply_ref[...] * own], axis=0), parts_ref
    )
    surface = answers[0:peers] + jnp.concatenate([bits(4), bits(5)], axis=1)
    cube_out_ref[0] = cube_ref[...] + answers[peers:]

    picked = dot(jnp.concatenate(parts_of(surface, 3), axis=0), at_node_ref[...])
    picked = picked[0:peers] + picked[peers : 2 * peers] + picked[2 * peers :]
    boundary = jnp.sum(picked * at_owner_ref[...].astype(jnp.float32), axis=0, keepdims=True)
    flux = interface_exchange * (boundary - warmth_ref[...])
    count = wide_x * wide_y
    at_plane = at_plane_ref[...]
    flux_parts = [
        at_plane * jnp.broadcast_to(part, at_plane.shape) for part in parts_of(flux, 3)
    ]
    gain = dot_last(jnp.concatenate(flux_parts, axis=0), at_depth_ref[...])
    gain = gain[0:count] + gain[count : 2 * count] + gain[2 * count :]
    for x in range(wide_x):
        rows = gain[x * wide_y : (x + 1) * wide_y]
        for i in range(7):
            heat_ref[i, x] = passed_ref[i, x] + thermal_stencil_coefficient[i] * rows


def call(kernel, shapes, *operands, smem=(), scratch=(), cost=1000000):
    spaces = [pltpu.SMEM if i in smem else pltpu.VMEM for i in range(len(operands))]
    moved = sum(4 * math.prod(o.shape) for o in list(operands) + list(shapes))
    return pl.pallas_call(
        kernel,
        out_shape=list(shapes),
        in_specs=[pl.BlockSpec(memory_space=space) for space in spaces],
        out_specs=[pl.BlockSpec(memory_space=pltpu.VMEM) for _ in shapes],
        scratch_shapes=list(scratch),
        compiler_params=pltpu.CompilerParams(vmem_limit_bytes=limit),
        cost_estimate=pl.CostEstimate(flops=cost, bytes_accessed=moved, transcendentals=0),
    )(*operands)


def f32(*shape):
    return jax.ShapeDtypeStruct(shape, jnp.float32)


def b16(*shape):
    return jax.ShapeDtypeStruct(shape, jnp.bfloat16)


def per_device(
    flow_state,
    thermal_distributions_current,
    fluid_mask,
    heat_rate,
    solid_source,
    cube_uptake_coefficients,
    owner_of,
    emitting_grid_site,
    target_node,
):
    bx, by, nz = fluid_mask.shape
    size, face = solid_source.shape[1:]
    peers, n_wide = lax.axis_size("narrow"), lax.axis_size("wide")
    rows = emitting_grid_site.shape[0]
    site = emitting_grid_site.reshape(2, rows // 2)
    owner = owner_of.reshape(2, rows // 2)
    node = target_node.reshape(2, rows // 2)
    me = lax.axis_index("narrow").astype(jnp.int32).reshape(1)
    wide = lax.axis_index("wide").astype(jnp.int32).reshape(1)
    sine, plane_parts, total, first = (jnp.asarray(c) for c in sine_constants(size))

    (early,) = call(
        first_kernel, (jax.ShapeDtypeStruct((8, nz), jnp.int32),), me, smem=(0,), cost=10**10
    )
    uptake = cube_uptake_coefficients.reshape(1, 1)
    post, heat_post, xa, xb, yu, yd, du, dd = call(
        collide_kernel,
        (
            f32(19, bx, by, nz), f32(7, bx, by, nz), f32(6, by, nz), f32(6, by, nz),
            f32(4, bx, nz), f32(4, bx, nz), f32(2, bx, nz), f32(2, bx, nz),
        ),
        me, flow_state, thermal_distributions_current, fluid_mask, heat_rate, early,
        solid_source, site, owner, node,
        smem=(0,),
    )
    part, at_plane, at_depth = call(
        functools.partial(face_kernel, n_wide=n_wide, face=face, depth=nz),
        (f32(8, face // 2), b16(bx * by, rows), b16(nz, rows)),
        solid_source, site, owner, node, uptake, wide, sine, plane_parts, total, first,
        smem=(5,),
        cost=10**10,
    )

    def send(block, axis, step):
        count = lax.axis_size(axis)
        return lax.ppermute(block, axis, [(i, (i + step) % count) for i in range(count)])

    def swap(block, start):
        low = range(start, peers, 2)
        pairs = [(i, (i + 1) % peers) for i in low] + [((i + 1) % peers, i) for i in low]
        return lax.ppermute(block, "narrow", pairs)

    xa = swap(xa, 1)
    yd, yu = send(yd, "wide", -1), send(yu, "wide", 1)
    xb = swap(xb, 0)
    passed, warmth, message = call(
        warmth_kernel,
        (f32(7, bx, by, nz), f32(1, rows), f32(peers, 8, face // 2)),
        me, heat_post, xa, yd, yu, xb, part, at_plane, at_depth,
        smem=(0,),
    )
    got = lax.all_to_all(message, "narrow", split_axis=0, concat_axis=0, tiled=True)
    du, dd = call(rim_kernel, (f32(2, bx, nz), f32(2, bx, nz)), me, du, dd, xa, xb, smem=(0,))
    dd, du = send(dd, "wide", -1), send(du, "wide", 1)
    (stream,) = call(
        stream_kernel, (f32(19, bx, by, nz),), me, post, xa, yd, yu, xb, dd, du, smem=(0,)
    )
    cube, reply, at_owner, at_node = call(
        block_kernel,
        (f32(size, face), f32(size, face), b16(peers, rows), b16(face, rows)),
        solid_source, owner, node, uptake, sine, plane_parts, total, first, du,
    )
    heat, cubes = call(
        functools.partial(finish_kernel, n_wide=n_wide, face=face),
        (f32(7, bx, by, nz), f32(1, size, face)),
        got.reshape(peers * 8, face // 2), passed, warmth, at_plane, at_depth, at_owner, at_node,
        me, cube, reply, plane_parts,
        smem=(7,),
        scratch=[pltpu.VMEM((2, peers, face // 2), jnp.float32)] * 3
        + [pltpu.VMEM((2, face // 2, peers), jnp.float32), pltpu.VMEM((peers, face), jnp.float32)],
    )
    return stream, heat, cubes


def solution(mesh):
    return jax.shard_map(
        per_device,
        mesh=mesh,
        in_specs=(
            P(None, "narrow", "wide", None),
            P(None, "narrow", "wide", None),
            P("narrow", "wide", None),
            P("narrow", "wide", None),
            P(("narrow", "wide"), None, None),
            P(("narrow", "wide")),
            P(("narrow", "wide"), None),
            P(("narrow", "wide")),
            P(("narrow", "wide")),
        ),
        out_specs=(
            P(None, "narrow", "wide", None),
            P(None, "narrow", "wide", None),
            P(("narrow", "wide"), None, None),
        ),
        check_vma=False,
    )
```

```python
import functools
import math

import jax
import jax.numpy as jnp
import numpy as np
from jax import lax
from jax.experimental import pallas as pl
from jax.experimental.pallas import tpu as pltpu
from jax.sharding import PartitionSpec as P

flow_velocity = np.array(
    [
        [0, 0, 0],
        [1, 0, 0],
        [-1, 0, 0],
        [0, 1, 0],
        [0, -1, 0],
        [0, 0, 1],
        [0, 0, -1],
        [1, 1, 0],
        [-1, -1, 0],
        [1, -1, 0],
        [-1, 1, 0],
        [1, 0, 1],
        [-1, 0, -1],
        [1, 0, -1],
        [-1, 0, 1],
        [0, 1, 1],
        [0, -1, -1],
        [0, 1, -1],
        [0, -1, 1],
    ],
    dtype=np.int32,
)
flow_opposite = [0, 2, 1, 4, 3, 6, 5, 8, 7, 10, 9, 12, 11, 14, 13, 16, 15, 18, 17]
flow_weight = [1.0 / 3.0] + [1.0 / 18.0] * 6 + [1.0 / 36.0] * 12
thermal_stencil_coefficient = [0.25] + [0.125] * 6
flow_rate = 1.2
interface_exchange = 0.5

x_up = (1, 7, 9, 11, 13)
x_down = (2, 8, 10, 12, 14)
y_up = (3, 15, 17)
y_down = (4, 16, 18)
diagonal_up = (7, 10)
diagonal_down = (8, 9)

HIGHEST = lax.Precision.HIGHEST
limit = 32 * 1024 * 1024


def sine_constants(size):
    counting = np.arange(1, size + 1, dtype=np.float64)
    sine = math.sqrt(2.0 / (size + 1)) * np.sin(
        math.pi * counting[:, None] * counting[None, :] / (size + 1)
    )
    values = 2.0 - 2.0 * np.cos(math.pi * counting / (size + 1))
    plane = np.kron(sine, sine)
    high = plane.astype(jnp.bfloat16)
    low = (plane - high.astype(np.float64)).astype(jnp.bfloat16)
    plane_parts = np.concatenate([high, high, low], axis=0)
    total = values[:, None] + (values[:, None] + values[None, :]).reshape(1, -1)
    return (
        sine.astype(np.float32),
        plane_parts,
        total.astype(np.float32),
        np.ascontiguousarray(np.broadcast_to(sine[:, :1], total.shape)).astype(np.float32),
    )


def dot(a, b, precision=None):
    return lax.dot_general(
        a, b, (((1,), (0,)), ((), ())), precision=precision, preferred_element_type=jnp.float32
    )


def dot_last(a, b):
    return lax.dot_general(a, b, (((1,), (1,)), ((), ())), preferred_element_type=jnp.float32)


def parts_of(value, count):
    parts = []
    for _ in range(count):
        part = value.astype(jnp.bfloat16)
        parts.append(part)
        value = value - part.astype(jnp.float32)
    return parts


def one_hot(row, size):
    numbers = lax.broadcasted_iota(jnp.int32, (size, row.shape[1]), 0)
    return jnp.where(numbers == row, 1.0, 0.0).astype(jnp.bfloat16)


def first_kernel(me_ref, out_ref):
    out_ref[...] = jnp.full(out_ref.shape, me_ref[0], jnp.int32)


def is_odd(me_ref, shape):
    return jnp.full(shape, me_ref[0] % 2, jnp.int32) == 1


def faces_along_x(me_ref, xa_ref, xb_ref):
    def pick(even_ref, odd_ref):
        def read(slot, rows=slice(None)):
            a, b = even_ref[slot, rows, :], odd_ref[slot, rows, :]
            return jnp.where(is_odd(me_ref, a.shape), b, a)

        return read

    return pick(xa_ref, xb_ref), pick(xb_ref, xa_ref)


def collide_kernel(me_ref, flow_ref, heat_ref, mask_ref, rate_ref, *refs):
    post_ref, heat_post_ref, xa_ref, xb_ref, yu_ref, yd_ref, du_ref, dd_ref = refs[-8:]
    wide_x, wide_y = flow_ref.shape[1], flow_ref.shape[2]
    for x in range(wide_x):
        f = [flow_ref[i, x] for i in range(19)]
        density = functools.reduce(lambda a, b: a + b, f)
        momentum = []
        for axis in range(3):
            plus = [f[i] for i in range(19) if flow_velocity[i, axis] > 0]
            minus = [f[i] for i in range(19) if flow_velocity[i, axis] < 0]
            momentum.append(
                functools.reduce(lambda a, b: a + b, plus)
                - functools.reduce(lambda a, b: a + b, minus)
            )
        speed = [m / density for m in momentum]
        square = speed[0] * speed[0] + speed[1] * speed[1] + speed[2] * speed[2]
        base = 1.0 - 1.5 * square
        is_fluid = mask_ref[x] == 1

        def along(i):
            total = None
            for axis in range(3):
                c = int(flow_velocity[i, axis])
                if c == 0:
                    continue
                term = speed[axis] if c > 0 else -speed[axis]
                total = term if total is None else total + term
            return total

        weighted = {w: density * w for w in set(flow_weight)}
        post = [None] * 19
        for i in [0] + list(range(1, 19, 2)):
            scale = weighted[flow_weight[i]]
            if i == 0:
                post[0] = jnp.where(is_fluid, f[0] - flow_rate * (f[0] - scale * base), f[0])
                continue
            cu = along(i)
            even = base + 4.5 * (cu * cu)
            odd = 3.0 * cu
            for k, balanced in ((i, scale * (even + odd)), (i + 1, scale * (even - odd))):
                post[k] = jnp.where(
                    is_fluid, f[k] - flow_rate * (f[k] - balanced), f[flow_opposite[k]]
                )
        h = [heat_ref[i, x] for i in range(7)]
        warmth = functools.reduce(lambda a, b: a + b, h)
        rate = rate_ref[x]
        heat = []
        for i in range(7):
            scale = thermal_stencil_coefficient[i] * warmth
            balanced = scale if i == 0 else scale * (1.0 + 4.0 * along(i))
            heat.append(jnp.where(is_fluid, h[i] - rate * (h[i] - balanced), h[flow_opposite[i]]))
        for i in range(19):
            post_ref[i, x] = post[i]
        for i in range(7):
            heat_post_ref[i, x] = heat[i]
        if x == 0:
            down = [heat[2]] + [post[i] for i in x_down]
        if x == wide_x - 1:
            odd = is_odd(me_ref, heat[1].shape)
            for slot, (low, high) in enumerate(zip(down, [heat[1]] + [post[i] for i in x_up])):
                xa_ref[slot] = jnp.where(odd, high, low)
                xb_ref[slot] = jnp.where(odd, low, high)
        last, row = slice(wide_y - 1, wide_y), slice(x, x + 1)
        for slot, part in enumerate([heat[3]] + [post[i] for i in y_up]):
            yu_ref[slot, row, :] = part[last]
        for slot, part in enumerate([heat[4]] + [post[i] for i in y_down]):
            yd_ref[slot, row, :] = part[0:1]
        for slot, i in enumerate(diagonal_up):
            du_ref[slot, row, :] = post[i][last]
        for slot, i in enumerate(diagonal_down):
            dd_ref[slot, row, :] = post[i][0:1]


def by_plane(value, parts_ref):
    high, low = parts_of(value, 2)
    return dot(jnp.concatenate([high, low, high], axis=1), parts_ref[...])


def flat(rows):
    return jnp.concatenate([rows[0:1], rows[1:2]], axis=1)


def face_kernel(
    source_ref, site_ref, owner_ref, node_ref, uptake_ref, wide_ref,
    sine_ref, parts_ref, total_ref, first_ref, part_ref, at_plane_ref, at_depth_ref,
    *, n_wide, face, depth,
):
    first = first_ref[...]
    inverse = 1.0 / (total_ref[...] + uptake_ref[...])
    spectral = by_plane(dot(sine_ref[...], source_ref[0], HIGHEST), parts_ref) * inverse
    reply = jnp.sum(first * first * inverse, axis=0, keepdims=True)
    answer = jnp.sum(first * spectral, axis=0, keepdims=True)
    answer = by_plane(jnp.broadcast_to(answer, (8, face)), parts_ref)[0:1]
    sites = site_ref[...]
    number = (owner_ref[...] * n_wide + wide_ref[0]) * face + node_ref[...]
    number = number.astype(jnp.float32)
    half = face // 2
    part_ref[...] = jnp.concatenate(
        [
            number, answer[:, 0:half], answer[:, half:], reply[:, 0:half], reply[:, half:],
            number,
        ],
        axis=0,
    )
    at_plane_ref[...] = one_hot(flat(sites // depth), at_plane_ref.shape[0])
    at_depth_ref[...] = one_hot(flat(sites % depth), at_depth_ref.shape[0])


def block_kernel(
    source_ref, owner_ref, node_ref, uptake_ref, sine_ref, parts_ref, total_ref, first_ref, _,
    cube_ref, reply_ref, at_owner_ref, at_node_ref,
):
    sine = sine_ref[...]
    inverse = 1.0 / (total_ref[...] + uptake_ref[...])
    spectral = by_plane(dot(sine, source_ref[0], HIGHEST), parts_ref) * inverse
    cube_ref[...] = by_plane(dot(sine, spectral, HIGHEST), parts_ref)
    reply_ref[...] = dot(sine, first_ref[...] * inverse, HIGHEST)
    at_owner_ref[...] = one_hot(flat(owner_ref[...]), at_owner_ref.shape[0])
    at_node_ref[...] = one_hot(flat(node_ref[...]), at_node_ref.shape[0])


def moved_x(rows, direction, edge):
    size = rows.shape[0]
    numbers = lax.broadcasted_iota(jnp.int32, rows.shape, 0)
    if direction > 0:
        return jnp.where(numbers == 0, edge, pltpu.roll(rows, 1, 0))
    return jnp.where(numbers == size - 1, edge, pltpu.roll(rows, size - 1, 0))


def rim_kernel(me_ref, du_raw_ref, dd_raw_ref, xa_ref, xb_ref, du_ref, dd_ref):
    last = xa_ref.shape[1] - 1
    below, above = faces_along_x(me_ref, xa_ref, xb_ref)
    for raw_ref, out_ref, names, y in (
        (du_raw_ref, du_ref, diagonal_up, last),
        (dd_raw_ref, dd_ref, diagonal_down, 0),
    ):
        for slot, i in enumerate(names):
            direction = int(flow_velocity[i, 0])
            face, at = (below, x_up) if direction > 0 else (above, x_down)
            edge = face(1 + at.index(i), slice(y, y + 1))
            out_ref[slot] = moved_x(raw_ref[slot], direction, edge)


def shifted_y(value, direction, edge):
    size = value.shape[0]
    rows = lax.broadcasted_iota(jnp.int32, value.shape, 0)
    if direction > 0:
        return jnp.where(rows == 0, edge, pltpu.roll(value, 1, 0))
    return jnp.where(rows == size - 1, edge, pltpu.roll(value, size - 1, 0))


def shifted_z(value, direction):
    if direction == 0:
        return value
    return pltpu.roll(value, 1 if direction > 0 else value.shape[1] - 1, 1)


def warmth_kernel(
    me_ref, heat_post_ref, xa_ref, yd_ref, yu_ref, xb_ref, part_ref, at_plane_ref, at_depth_ref,
    passed_ref, warmth_ref, send_ref,
):
    wide_x, wide_y, depth = heat_post_ref.shape[1:]
    below, above = faces_along_x(me_ref, xa_ref, xb_ref)
    planes = []
    for x in range(wide_x):
        passed = [
            heat_post_ref[0, x],
            below(0) if x == 0 else heat_post_ref[1, x - 1],
            above(0) if x == wide_x - 1 else heat_post_ref[2, x + 1],
            shifted_y(heat_post_ref[3, x], 1, yu_ref[0, x : x + 1, :]),
            shifted_y(heat_post_ref[4, x], -1, yd_ref[0, x : x + 1, :]),
            shifted_z(heat_post_ref[5, x], 1),
            shifted_z(heat_post_ref[6, x], -1),
        ]
        for i in range(7):
            passed_ref[i, x] = passed[i]
        planes.append(functools.reduce(lambda a, b: a + b, passed))
    field = jnp.concatenate(planes, axis=0)
    count = wide_x * wide_y
    picked = dot(jnp.concatenate(parts_of(field, 3), axis=0), at_depth_ref[...])
    picked = picked[0:count] + picked[count : 2 * count] + picked[2 * count :]
    warmth = jnp.sum(picked * at_plane_ref[...].astype(jnp.float32), axis=0, keepdims=True)
    warmth_ref[...] = warmth
    half = warmth.shape[1] // 2
    message = jnp.concatenate([warmth[:, 0:half], warmth[:, half:], part_ref[0:6]], axis=0)
    for peer in range(send_ref.shape[0]):
        send_ref[peer] = message


def stream_kernel(
    me_ref, post_ref, xa_ref, yd_ref, yu_ref, xb_ref, dd_ref, du_ref, out_ref
):
    below, above = faces_along_x(me_ref, xa_ref, xb_ref)
    wide_x = post_ref.shape[1]
    for i in range(19):
        cx, cy, cz = (int(c) for c in flow_velocity[i])
        for x in range(wide_x):
            if cx > 0 and x == 0:
                value = below(1 + x_up.index(i))
            elif cx < 0 and x == wide_x - 1:
                value = above(1 + x_down.index(i))
            else:
                value = post_ref[i, x - cx]
            if cy:
                if cx:
                    edges = du_ref if cy > 0 else dd_ref
                    slot = (diagonal_up if cy > 0 else diagonal_down).index(i)
                else:
                    edges = yu_ref if cy > 0 else yd_ref
                    slot = 1 + (y_up if cy > 0 else y_down).index(i)
                value = shifted_y(value, cy, edges[slot, x : x + 1, :])
            out_ref[i, x] = shifted_z(value, cz)


def finish_kernel(
    got_ref, passed_ref, warmth_ref, at_plane_ref, at_depth_ref, at_owner_ref, at_node_ref,
    me_ref, cube_ref, reply_ref, parts_ref,
    heat_ref, cube_out_ref,
    high_ref, low_ref, owner_rows_ref, node_columns_ref, table_ref, *, n_wide, face,
):
    peers, depth = got_ref.shape[0] // 8, got_ref.shape[1]
    wide_x, wide_y = passed_ref.shape[1:3]
    bits = lambda row: got_ref[pl.ds(row, peers, stride=8), :]
    for half in range(2):
        temperature = bits(half)
        high = temperature.astype(jnp.bfloat16).astype(jnp.float32)
        high_ref[half] = high
        low_ref[half] = temperature - high
        number = bits(2 + half).astype(jnp.int32)
        owner_rows_ref[half] = (number // (n_wide * face)).astype(jnp.float32)
        node_columns_ref[half] = (number % face).astype(jnp.float32).T

    def spread(ref, half, d):
        row = ref[half, d : d + 1, :]
        return jnp.broadcast_to(row, (16, depth)).astype(jnp.bfloat16)

    numbers = lax.broadcasted_iota(jnp.int32, (16, depth), 0).astype(jnp.float32)
    lanes = lax.broadcasted_iota(jnp.int32, (depth, face), 1).astype(jnp.float32)
    lanes = lanes.astype(jnp.bfloat16)
    zero, one = jnp.bfloat16(0), jnp.bfloat16(1)
    owner_groups = -(-peers // 16)
    wanted = [(numbers + 16.0 * g).astype(jnp.bfloat16) for g in range(owner_groups)]
    both = jnp.zeros((2 * 16 * owner_groups, face), jnp.float32)
    chunk = math.gcd(peers, 8)
    for start in range(0, peers, chunk):
        left, right = [], []
        for d in range(start, start + chunk):
            for half in range(2):
                owner = spread(owner_rows_ref, half, d)
                high, low = spread(high_ref, half, d), spread(low_ref, half, d)
                hits = [owner == w for w in wanted]
                left.append(
                    jnp.concatenate(
                        [jnp.where(hit, high, zero) for hit in hits]
                        + [jnp.where(hit, low, zero) for hit in hits],
                        axis=0,
                    )
                )
                node = node_columns_ref[half, :, d : d + 1].astype(jnp.bfloat16)
                hit = jnp.broadcast_to(node, (depth, face)) == lanes
                right.append(jnp.where(hit, one, zero))
        both = both + dot(jnp.concatenate(left, axis=1), jnp.concatenate(right, axis=0))
    table = interface_exchange * (both[0:peers] + both[16 * owner_groups :][0:peers])
    spectral = by_plane(table, parts_ref)
    table_ref[...] = spectral
    reply = jnp.concatenate([bits(6), bits(7)], axis=1)
    own = table_ref[pl.ds(me_ref[0], 1), :]
    answers = by_plane(
        jnp.concatenate([spectral * reply, reply_ref[...] * own], axis=0), parts_ref
    )
    surface = answers[0:peers] + jnp.concatenate([bits(4), bits(5)], axis=1)
    cube_out_ref[0] = cube_ref[...] + answers[peers:]

    picked = dot(jnp.concatenate(parts_of(surface, 3), axis=0), at_node_ref[...])
    picked = picked[0:peers] + picked[peers : 2 * peers] + picked[2 * peers :]
    boundary = jnp.sum(picked * at_owner_ref[...].astype(jnp.float32), axis=0, keepdims=True)
    flux = interface_exchange * (boundary - warmth_ref[...])
    count = wide_x * wide_y
    at_plane = at_plane_ref[...]
    flux_parts = [
        at_plane * jnp.broadcast_to(part, at_plane.shape) for part in parts_of(flux, 3)
    ]
    gain = dot_last(jnp.concatenate(flux_parts, axis=0), at_depth_ref[...])
    gain = gain[0:count] + gain[count : 2 * count] + gain[2 * count :]
    for x in range(wide_x):
        rows = gain[x * wide_y : (x + 1) * wide_y]
        for i in range(7):
            heat_ref[i, x] = passed_ref[i, x] + thermal_stencil_coefficient[i] * rows


def call(kernel, shapes, *operands, smem=(), scratch=(), cost=1000000):
    spaces = [pltpu.SMEM if i in smem else pltpu.VMEM for i in range(len(operands))]
    moved = sum(4 * math.prod(o.shape) for o in list(operands) + list(shapes))
    return pl.pallas_call(
        kernel,
        out_shape=list(shapes),
        in_specs=[pl.BlockSpec(memory_space=space) for space in spaces],
        out_specs=[pl.BlockSpec(memory_space=pltpu.VMEM) for _ in shapes],
        scratch_shapes=list(scratch),
        compiler_params=pltpu.CompilerParams(vmem_limit_bytes=limit),
        cost_estimate=pl.CostEstimate(flops=cost, bytes_accessed=moved, transcendentals=0),
    )(*operands)


def f32(*shape):
    return jax.ShapeDtypeStruct(shape, jnp.float32)


def b16(*shape):
    return jax.ShapeDtypeStruct(shape, jnp.bfloat16)


def per_device(
    flow_state,
    thermal_distributions_current,
    fluid_mask,
    heat_rate,
    solid_source,
    cube_uptake_coefficients,
    owner_of,
    emitting_grid_site,
    target_node,
):
    bx, by, nz = fluid_mask.shape
    size, face = solid_source.shape[1:]
    peers, n_wide = lax.axis_size("narrow"), lax.axis_size("wide")
    rows = emitting_grid_site.shape[0]
    site = emitting_grid_site.reshape(2, rows // 2)
    owner = owner_of.reshape(2, rows // 2)
    node = target_node.reshape(2, rows // 2)
    me = lax.axis_index("narrow").astype(jnp.int32).reshape(1)
    wide = lax.axis_index("wide").astype(jnp.int32).reshape(1)
    sine, plane_parts, total, first = (jnp.asarray(c) for c in sine_constants(size))

    (early,) = call(
        first_kernel, (jax.ShapeDtypeStruct((8, nz), jnp.int32),), me, smem=(0,), cost=10**10
    )
    uptake = cube_uptake_coefficients.reshape(1, 1)
    post, heat_post, xa, xb, yu, yd, du, dd = call(
        collide_kernel,
        (
            f32(19, bx, by, nz), f32(7, bx, by, nz), f32(6, by, nz), f32(6, by, nz),
            f32(4, bx, nz), f32(4, bx, nz), f32(2, bx, nz), f32(2, bx, nz),
        ),
        me, flow_state, thermal_distributions_current, fluid_mask, heat_rate, early,
        solid_source, site, owner, node,
        smem=(0,),
    )
    part, at_plane, at_depth = call(
        functools.partial(face_kernel, n_wide=n_wide, face=face, depth=nz),
        (f32(8, face // 2), b16(bx * by, rows), b16(nz, rows)),
        solid_source, site, owner, node, uptake, wide, sine, plane_parts, total, first,
        smem=(5,),
        cost=10**10,
    )

    def send(block, axis, step):
        count = lax.axis_size(axis)
        return lax.ppermute(block, axis, [(i, (i + step) % count) for i in range(count)])

    def swap(block, start):
        low = range(start, peers, 2)
        pairs = [(i, (i + 1) % peers) for i in low] + [((i + 1) % peers, i) for i in low]
        return lax.ppermute(block, "narrow", pairs)

    xa = swap(xa, 1)
    yd, yu = send(yd, "wide", -1), send(yu, "wide", 1)
    xb = swap(xb, 0)
    passed, warmth, message = call(
        warmth_kernel,
        (f32(7, bx, by, nz), f32(1, rows), f32(peers, 8, face // 2)),
        me, heat_post, xa, yd, yu, xb, part, at_plane, at_depth,
        smem=(0,),
    )
    got = lax.all_to_all(message, "narrow", split_axis=0, concat_axis=0, tiled=True)
    du, dd = call(rim_kernel, (f32(2, bx, nz), f32(2, bx, nz)), me, du, dd, xa, xb, smem=(0,))
    dd, du = send(dd, "wide", -1), send(du, "wide", 1)
    (stream,) = call(
        stream_kernel, (f32(19, bx, by, nz),), me, post, xa, yd, yu, xb, dd, du, smem=(0,)
    )
    cube, reply, at_owner, at_node = call(
        block_kernel,
        (f32(size, face), f32(size, face), b16(peers, rows), b16(face, rows)),
        solid_source, owner, node, uptake, sine, plane_parts, total, first, du,
    )
    heat, cubes = call(
        functools.partial(finish_kernel, n_wide=n_wide, face=face),
        (f32(7, bx, by, nz), f32(1, size, face)),
        got.reshape(peers * 8, face // 2), passed, warmth, at_plane, at_depth, at_owner, at_node,
        me, cube, reply, plane_parts,
        smem=(7,),
        scratch=[pltpu.VMEM((2, peers, face // 2), jnp.float32)] * 3
        + [pltpu.VMEM((2, face // 2, peers), jnp.float32), pltpu.VMEM((peers, face), jnp.float32)],
    )
    return stream, heat, cubes


def solution(mesh):
    return jax.shard_map(
        per_device,
        mesh=mesh,
        in_specs=(
            P(None, "narrow", "wide", None),
            P(None, "narrow", "wide", None),
            P("narrow", "wide", None),
            P("narrow", "wide", None),
            P(("narrow", "wide"), None, None),
            P(("narrow", "wide")),
            P(("narrow", "wide"), None),
            P(("narrow", "wide")),
            P(("narrow", "wide")),
        ),
        out_specs=(
            P(None, "narrow", "wide", None),
            P(None, "narrow", "wide", None),
            P(("narrow", "wide"), None, None),
        ),
        check_vma=False,
    )
```
